512 devices in a mesh: lon: 32 (over z_hi, x, core), lat: 16 (over y, z_lo).
Axes of the slice: x: 4, y: 8, z: 8 (z_hi: 4, z_lo: 2; z = z_hi * 2 + z_lo), core: 2. Of those that a mesh axis runs over, the one named last changes fastest.
Arguments:
- fields: bfloat16 [96, 128, 8192], P(None, 'lat', 'lon'), may hold values from -6 to 6
- land_mask: int32 [128, 8192], P('lat', 'lon'), may hold values from 0 to 1, as said below
- dw_kernel: float32 [96, 7, 7], replicated, may hold values from -0.875 to 0.875
- gain: float32 [96], replicated, may hold values from 0.1 to 1.9
- w_in: bfloat16 [96, 192], replicated, may hold values from -0.625 to 0.625
- b_in: float32 [192], replicated, may hold values from -3 to 3
- w_out: bfloat16 [192, 96], replicated, may hold values from -0.4375 to 0.4375
- cotangent: bfloat16 [96, 128, 8192], P(None, 'lat', 'lon'), may hold values from -6 to 6
Outputs:
- output: bfloat16 [96, 128, 8192], P(None, 'lat', 'lon')
- input_grad: bfloat16 [96, 128, 8192], P(None, 'lat', 'lon')
- kernel_grad: float32 [96, 7, 7], replicated
- gain_grad: float32 [96], replicated
- w_in_grad: float32 [96, 192], replicated
- b_in_grad: float32 [192], replicated
- w_out_grad: float32 [192, 96], replicated
The draws below stay inside these ranges and needn't reach their ends.
Inputs may be any that keep to these rules, and one draw needn't show every extreme that they name: `land_mask`: 1 marks a sea cell and 0 a land cell.
All inputs are finite; a program needn't handle non-finite values.
Results may differ from the reference program's by a relative error of at most 0.009.
Values may be sent and summed in bfloat16 or wider, within the bound.
No kernel may reach another device: no remote copies, remote signals or barrier semaphores. Data moves between devices by JAX's collectives and lax.ppermute only.
A program may use at most 192 MiB of HBM per device.

```python
import jax
import jax.numpy as jnp
from jax import lax

C = 96
H = 192
CLAT = 8
CLON = 256
NLAT = 128
NLON = 8192


def draw_land_mask(key, part):
    levels_key, cell_key = jax.random.split(jax.random.fold_in(key, 11))
    block_rows = CLAT // 2
    block_cols = CLON // 2
    levels = jax.random.randint(levels_key, (NLAT // block_rows, NLON // block_cols), 0, 4)
    limits = jnp.array([10, 35, 65, 100], jnp.int32)[levels]
    limits = jnp.repeat(jnp.repeat(limits, block_rows, axis=0), block_cols, axis=1)
    cell_draws = jax.random.randint(cell_key, (NLAT, NLON), 0, 100)
    return (cell_draws >= limits).astype(jnp.int32)


def level_of(own_key, extent, cuts, low, high):
    def one(axis_at, shards_of):
        draws = jax.random.uniform(jax.random.fold_in(jax.random.fold_in(own_key, 6), axis_at), (shards_of,), jnp.float32, low / len(cuts), high / len(cuts))
        return jnp.repeat(jnp.exp(draws), extent[axis_at] // shards_of).reshape((-1,) + (1,) * (len(extent) - axis_at - 1))

    loudness = one(*cuts[0])
    for cut in cuts[1:]:
        loudness = loudness * one(*cut)
    return loudness


def scatter_about(own_key, extent, deviation, most, shards=(), held_as=jnp.bfloat16):
    values = deviation * jax.random.normal(own_key, extent, jnp.float32)
    if shards:
        values = values * level_of(own_key, extent, shards, -0.22, 0.18)
    return jnp.clip(values, -most, most).astype(held_as)


def setup_inputs(seed: int = 0) -> dict:
    keys = jax.random.split(jax.random.key(seed), 9)
    fields = scatter_about(keys[0], (C, NLAT, NLON), 1.0, 6.0, ((1, 16), (2, 32)))
    land_mask = draw_land_mask(jax.random.fold_in(keys[8], 71), 0)
    dw_kernel = scatter_about(keys[2], (C, 7, 7), 49 ** -0.5, 0.875, (), jnp.float32)
    gain = jnp.clip(1.0 + 0.18 * jax.random.normal(keys[3], (C,), jnp.float32), 0.1, 1.9)
    w_in = scatter_about(keys[4], (C, H), C ** -0.5, 0.625)
    b_in = scatter_about(keys[5], (H,), 0.5, 3.0, (), jnp.float32)
    w_out = scatter_about(keys[6], (H, C), H ** -0.5, 0.4375)
    cotangent = scatter_about(keys[7], (C, NLAT, NLON), 1.0, 6.0, ((1, 16), (2, 32)))
    return dict(fields=fields, land_mask=land_mask, dw_kernel=dw_kernel, gain=gain, w_in=w_in, b_in=b_in, w_out=w_out, cotangent=cotangent)


def extend(values):
    wide = jnp.concatenate([values[:, :, -3:], values, values[:, :, :3]], axis=2)
    north = wide[:, ::-1, ::-1][:, :3, :]
    south = jnp.zeros_like(wide[:, :3, :])
    return jnp.concatenate([south, wide, north], axis=1)

def retract(grads):
    inner = grads[:, 3:-3, :]
    north = grads[:, -3:, :]
    inner = inner.at[:, -3:, :].add(north[:, ::-1, ::-1])
    core = inner[:, :, 3:-3]
    core = core.at[:, :, :3].add(inner[:, :, -3:])
    core = core.at[:, :, -3:].add(inner[:, :, :3])
    return core

def convolve(padded, kernel, tile_rows, tile_cols):
    summed = jnp.zeros((padded.shape[0], tile_rows, tile_cols), jnp.float32)
    for row_off in range(7):
        for col_off in range(7):
            window = padded[:, row_off:row_off + tile_rows, col_off:col_off + tile_cols].astype(jnp.float32)
            summed = summed + kernel[:, row_off, col_off][:, None, None] * window
    return summed

def spread_back(conv_grad, kernel):
    channels, tile_rows, tile_cols = conv_grad.shape
    bordered = jnp.pad(conv_grad, ((0, 0), (6, 6), (6, 6)))
    summed = jnp.zeros((channels, tile_rows + 6, tile_cols + 6), jnp.float32)
    for row_off in range(7):
        for col_off in range(7):
            window = bordered[:, 6 - row_off:12 - row_off + tile_rows, 6 - col_off:12 - col_off + tile_cols]
            summed = summed + kernel[:, row_off, col_off][:, None, None] * window
    return summed

def kernel_terms(conv_grad, padded):
    channels, tile_rows, tile_cols = conv_grad.shape
    terms = []
    for row_off in range(7):
        for col_off in range(7):
            window = padded[:, row_off:row_off + tile_rows, col_off:col_off + tile_cols].astype(jnp.float32)
            terms.append(lax.optimization_barrier(jnp.sum(conv_grad * window, axis=(1, 2))))
    return jnp.stack(terms, axis=1).reshape(channels, 7, 7)

def reference(fields, land_mask, dw_kernel, gain, w_in, b_in, w_out, cotangent):
    highest = lax.Precision.HIGHEST
    sea_mask = land_mask.astype(jnp.bfloat16)[None]
    masked = fields * sea_mask
    back_all = cotangent * sea_mask
    padded = extend(masked)
    w_in_wide = w_in.astype(jnp.float32)
    w_out_wide = w_out.astype(jnp.float32)

    def scan_step(running, block):
        ext_grad, kernel_acc, gain_acc, w_in_acc, b_acc, w_out_acc = running
        start = (block * CLAT).astype(jnp.int32)
        piece = lax.dynamic_slice_in_dim(padded, start, CLAT + 6, axis=1)
        sea_part = lax.dynamic_slice_in_dim(sea_mask, start, CLAT, axis=1)
        back_part = lax.dynamic_slice_in_dim(back_all, start, CLAT, axis=1)
        conv_out = convolve(piece, dw_kernel, CLAT, NLON)
        centred = conv_out - lax.optimization_barrier(jnp.mean(conv_out, axis=0, keepdims=True))
        inv_std = lax.rsqrt(lax.optimization_barrier(jnp.mean(centred * centred, axis=0, keepdims=True)) + 1e-06)
        normed = centred * inv_std
        scaled = (normed * gain[:, None, None]).astype(jnp.bfloat16)
        hidden_pre = jnp.einsum('ch,cxy->hxy', w_in_wide, scaled.astype(jnp.float32), precision=highest) + b_in[:, None, None]
        activated, gelu_pull = jax.vjp(jax.nn.gelu, hidden_pre)
        activated = activated.astype(jnp.bfloat16)
        act_wide = activated.astype(jnp.float32)
        mixed = jnp.einsum('hc,hxy->cxy', w_out_wide, act_wide, precision=highest)
        centre = piece[:, 3:CLAT + 3, 3:NLON + 3].astype(jnp.float32)
        output_part = (sea_part * (centre + mixed)).astype(jnp.bfloat16)
        back_wide = back_part.astype(jnp.float32)
        w_out_part = jnp.einsum('hxy,cxy->hc', act_wide, back_wide, precision=highest)
        act_grad = jnp.einsum('hc,cxy->hxy', w_out_wide, back_wide, precision=highest)
        pre_grad = gelu_pull(act_grad)[0].astype(jnp.bfloat16)
        pre_wide = pre_grad.astype(jnp.float32)
        b_part = lax.optimization_barrier(jnp.sum(pre_wide, axis=(1, 2)))
        w_in_part = jnp.einsum('cxy,hxy->ch', scaled.astype(jnp.float32), pre_wide, precision=highest)
        scaled_grad = jnp.einsum('ch,hxy->cxy', w_in_wide, pre_wide, precision=highest)
        gain_part = lax.optimization_barrier(jnp.sum(scaled_grad * normed, axis=(1, 2)))
        norm_grad = scaled_grad * gain[:, None, None]
        conv_grad = inv_std * (norm_grad - lax.optimization_barrier(jnp.mean(norm_grad, axis=0, keepdims=True)) - normed * lax.optimization_barrier(jnp.mean(norm_grad * normed, axis=0, keepdims=True)))
        kernel_part = kernel_terms(conv_grad, piece)
        previous = lax.dynamic_slice_in_dim(ext_grad, start, CLAT + 6, axis=1)
        ext_grad = lax.dynamic_update_slice_in_dim(ext_grad, previous + spread_back(conv_grad, dw_kernel), start, axis=1)
        running = (ext_grad, kernel_acc + kernel_part, gain_acc + gain_part, w_in_acc + w_in_part, b_acc + b_part, w_out_acc + w_out_part)
        return (running, output_part)
    initial = (jnp.zeros((C, NLAT + 6, NLON + 6), jnp.float32), jnp.zeros((C, 7, 7), jnp.float32), jnp.zeros((C,), jnp.float32), jnp.zeros((C, H), jnp.float32), jnp.zeros((H,), jnp.float32), jnp.zeros((H, C), jnp.float32))
    running, pieces = lax.scan(scan_step, initial, jnp.arange(NLAT // CLAT, dtype=jnp.int32))
    ext_grad, kernel_acc, gain_acc, w_in_acc, b_acc, w_out_acc = running
    output = jnp.transpose(pieces, (1, 0, 2, 3)).reshape(C, NLAT, NLON)
    masked_grad = retract(ext_grad)
    input_grad = (sea_mask * (masked_grad + back_all.astype(jnp.float32))).astype(jnp.bfloat16)
    scale_factor = float(NLAT * NLON) ** (-0.5)
    return (output, input_grad, kernel_acc * scale_factor, gain_acc * scale_factor, w_in_acc * scale_factor, b_acc * scale_factor, w_out_acc * scale_factor)
```

```python
import functools

import jax
import jax.numpy as jnp
from jax import lax
from jax.experimental import pallas as pl
from jax.experimental.pallas import tpu as pltpu
from jax.sharding import PartitionSpec as P

F32 = jnp.float32
BF16 = jnp.bfloat16
VMEM_LIMIT = 56 * 1024 * 1024
RING = 3


def call(body, outs, *args, scratch=()):
    return pl.pallas_call(
        body,
        out_shape=outs,
        in_specs=[pl.BlockSpec(memory_space=pltpu.VMEM)] * len(args),
        out_specs=[pl.BlockSpec(memory_space=pltpu.VMEM)] * len(outs),
        scratch_shapes=list(scratch),
        compiler_params=pltpu.CompilerParams(vmem_limit_bytes=VMEM_LIMIT),
    )(*args)


def lanes():
    return lax.broadcasted_iota(jnp.int32, (8, 128), 1)


def spread(flat, values):
    channels, rows, cols = values.shape
    for t in range(cols // 128):
        part = values[:, :, t * 128 : t * 128 + 128]
        flat[t] = part.reshape(channels * rows, 128)


def gather(flat, channels, rows):
    parts = [flat[t].reshape(channels, rows, 128) for t in range(flat.shape[0])]
    return jnp.concatenate(parts, axis=2)


def row_of(flat, i, channels, rows):
    parts = [flat[t, pl.ds(i, channels, stride=rows), :] for t in range(flat.shape[0])]
    return jnp.concatenate(parts, axis=1)


def rows_body(f_ref, mask_ref, m_ref, first_ref, last_ref, flat):
    channels, rows, cols = f_ref.shape
    sea = mask_ref[...].astype(F32)
    spread(flat, f_ref[...].astype(F32) * sea[None])
    for i in range(rows):
        row = row_of(flat, i, channels, rows).astype(BF16)
        m_ref[i] = row
        if i < RING:
            first_ref[i] = row
        if i >= rows - RING:
            last_ref[i - (rows - RING)] = row


def strips_body(m_ref, south_ref, north_ref, mirror_ref, flip_ref, halo_ref, left_ref, right_ref):
    rows, channels, cols = m_ref.shape
    for k in range(RING):
        turned = jnp.dot(mirror_ref[RING - 1 - k], flip_ref[...], preferred_element_type=F32)
        halo_ref[k] = (north_ref[k].astype(F32) + turned).astype(BF16)
    lane = lax.broadcasted_iota(jnp.int32, (channels, 128), 1)
    left = jnp.zeros((channels, 128), F32)
    right = jnp.zeros((channels, 128), F32)
    for r in range(rows + 2 * RING):
        if r < RING:
            ref, at = south_ref, r
        elif r < rows + RING:
            ref, at = m_ref, r - RING
        else:
            ref, at = halo_ref, r - RING - rows
        here = (lane >= RING * r) & (lane < RING * r + RING)
        head = ref[at, :, 0:128].astype(F32)
        tail = ref[at, :, cols - 128 : cols].astype(F32)
        if r:
            head = pltpu.roll(head, RING * r, 1)
        tail = pltpu.roll(tail, RING * r + RING, 1)
        left = jnp.where(here, head, left)
        right = jnp.where(here, tail, right)
    left_ref[...] = left.astype(BF16)
    right_ref[...] = right.astype(BF16)


def fill(ext, m_ref, south_ref, halo_ref, before_ref, after_ref):
    rows, channels, cols = m_ref.shape
    lane = lax.broadcasted_iota(jnp.int32, (channels, 128), 1)
    before = before_ref[...].astype(F32)
    after = after_ref[...].astype(F32)
    for r in range(rows + 2 * RING):
        if r < RING:
            row = south_ref[r]
        elif r < rows + RING:
            row = m_ref[r - RING]
        else:
            row = halo_ref[r - RING - rows]
        ext[r, :, 0:cols] = row.astype(F32)
        right = after if r == 0 else pltpu.roll(after, 128 - RING * r, 1)
        left = pltpu.roll(before, 128 - RING - RING * r, 1)
        ext[r, :, cols : cols + 128] = jnp.where(
            lane < RING, right, jnp.where(lane >= 128 - RING, left, 0.0)
        )


def windows(tiles, step, lane):
    if step == 0:
        return tiles[:-1]
    count = len(tiles)
    if step > 0:
        turned = [pltpu.roll(t, 128 - step, 1) for t in tiles]
        keep = lane < 128 - step
        return [jnp.where(keep, turned[t], turned[t + 1]) for t in range(count - 1)]
    turned = [pltpu.roll(t, -step, 1) for t in tiles]
    keep = lane >= -step
    return [jnp.where(keep, turned[t], turned[t - 1]) for t in range(count - 1)]


def tap(weights, index):
    return jnp.broadcast_to(weights[:, index : index + 1], (8, 128))


def correlate(ext, c0, rows, pairs, lane, weights, north):
    summed = [[None] * pairs for _ in range(rows)]
    for b in range(7):
        taps = [tap(weights, a * 7 + b) for a in range(7)]
        far = taps if north is None else [tap(north, a * 7 + b) for a in range(7)]
        for r in range(rows + 2 * RING):
            tiles = [ext[r, pl.ds(c0, 8), t * 128 : t * 128 + 128] for t in range(pairs + 1)]
            wins = windows(tiles, b - RING, lane)
            for a in range(7):
                i = r - a
                if 0 <= i < rows:
                    weight = far[a] if r >= rows + RING else taps[a]
                    for t in range(pairs):
                        term = weight * wins[t]
                        old = summed[i][t]
                        summed[i][t] = term if old is None else old + term
    return summed


def block_body(
    m_ref, south_ref, halo_ref, before_ref, after_ref, ct_ref, mask_ref,
    dw_ref, gain_ref, w_in_ref, w_in_t_ref, b_ref, w_out_ref, w_out_t_ref,
    out_ref, g_ref, first_ref, last_ref, sums_ref,
    ext, conv, flat, act, back, sca, pre, b_acc, gain_acc,
):
    rows, channels, cols = m_ref.shape
    hidden = w_out_ref.shape[0]
    pairs = cols // 128
    fill(ext, m_ref, south_ref, halo_ref, before_ref, after_ref)
    sea = mask_ref[...].astype(F32)
    spread(flat, ct_ref[...].astype(F32) * sea[None])
    for i in range(rows):
        back[:, i * cols : i * cols + cols] = row_of(flat, i, channels, rows).astype(BF16)

    def conv_step(ct, carry):
        c0 = pl.multiple_of(ct * 8, 8)
        lane = lanes()
        summed = correlate(ext, c0, rows, pairs, lane, dw_ref[pl.ds(c0, 8), :], None)
        for i in range(rows):
            for t in range(pairs):
                conv[i, pl.ds(c0, 8), t * 128 : t * 128 + 128] = summed[i][t]
        return carry

    lax.fori_loop(0, channels // 8, conv_step, 0)

    b_acc[...] = jnp.zeros_like(b_acc)
    gain_acc[...] = jnp.zeros_like(gain_acc)
    gain = jnp.broadcast_to(gain_ref[...], (channels, cols))
    bias = jnp.broadcast_to(b_ref[...], (hidden, cols))
    root = 0.7978845608028654
    for i in range(rows):
        span = slice(i * cols, i * cols + cols)
        raw = conv[i]
        centred = raw - jnp.mean(raw, axis=0, keepdims=True)
        inv_std = lax.rsqrt(jnp.mean(centred * centred, axis=0, keepdims=True) + 1e-06)
        normed = centred * inv_std
        scaled = (normed * gain).astype(BF16)
        sca[:, span] = scaled
        v = jnp.dot(w_in_t_ref[...], scaled, preferred_element_type=F32) + bias
        v2 = v * v
        t = jnp.tanh(root * v * (1.0 + 0.044715 * v2))
        half = 0.5 * (1.0 + t)
        activated = (v * half).astype(BF16)
        act[:, span] = activated
        slope = half + 0.5 * v * (1.0 - t * t) * (root * (1.0 + 3 * 0.044715 * v2))
        mixed = jnp.dot(w_out_t_ref[...], activated, preferred_element_type=F32)
        mixed = m_ref[i].astype(F32) + mixed
        for t in range(pairs):
            flat[t, pl.ds(i, channels, stride=rows), :] = mixed[:, t * 128 : t * 128 + 128]
        act_grad = jnp.dot(w_out_ref[...], back[:, span], preferred_element_type=F32)
        pre_grad = (act_grad * slope).astype(BF16)
        pre[:, span] = pre_grad
        wide = pre_grad.astype(F32)
        b_acc[...] += sum(wide[:, t * 128 : t * 128 + 128] for t in range(pairs))
        scaled_grad = jnp.dot(w_in_ref[...], pre_grad, preferred_element_type=F32)
        gains = scaled_grad * normed
        gain_acc[...] += sum(gains[:, t * 128 : t * 128 + 128] for t in range(pairs))
        norm_grad = scaled_grad * gain
        grad = inv_std * (
            norm_grad
            - jnp.mean(norm_grad, axis=0, keepdims=True)
            - normed * jnp.mean(norm_grad * normed, axis=0, keepdims=True)
        )
        conv[i] = grad
        short = grad.astype(BF16)
        g_ref[i] = short
        if i < RING:
            first_ref[i] = short
        if i >= rows - RING:
            last_ref[i - (rows - RING)] = short

    out_ref[...] = (gather(flat, channels, rows) * sea[None]).astype(BF16)
    over_cells = (((1,), (1,)), ((), ()))
    w_in_sum = lax.dot_general(sca[...], pre[...], over_cells, preferred_element_type=F32)
    w_out_sum = lax.dot_general(act[...], back[...], over_cells, preferred_element_type=F32)
    sums_ref[0:channels, :] = w_in_sum[:, 0:128]
    sums_ref[channels : channels + hidden, :] = jnp.zeros((hidden, 128), F32)
    sums_ref[channels : channels + hidden, 0:channels] = w_out_sum
    low = channels + hidden
    sums_ref[low : low + channels, :] = jnp.zeros((channels, 128), F32)
    sums_ref[low : low + channels, 0 : hidden - 128] = w_in_sum[:, 128:hidden]
    shift = hidden - 128

    def kernel_step(ct, carry):
        c0 = pl.multiple_of(ct * 8, 8)
        lane = lanes()
        at = pl.multiple_of(low + c0, 8)
        tile = sums_ref[pl.ds(at, 8), :]
        grads = [
            [conv[i, pl.ds(c0, 8), t * 128 : t * 128 + 128] for t in range(pairs)]
            for i in range(rows)
        ]
        for b in range(7):
            summed = [None] * 7
            for r in range(rows + 2 * RING):
                tiles = [ext[r, pl.ds(c0, 8), t * 128 : t * 128 + 128] for t in range(pairs + 1)]
                wins = windows(tiles, b - RING, lane)
                for a in range(7):
                    i = r - a
                    if 0 <= i < rows:
                        for t in range(pairs):
                            term = grads[i][t] * wins[t]
                            summed[a] = term if summed[a] is None else summed[a] + term
            for a in range(7):
                total = jnp.sum(summed[a], axis=1, keepdims=True)
                tile = jnp.where(lane == shift + a * 7 + b, total, tile)
        total = jnp.sum(gain_acc[pl.ds(c0, 8), :], axis=1, keepdims=True)
        tile = jnp.where(lane == shift + 49, total, tile)
        for part in range(hidden // channels):
            start = pl.multiple_of(part * channels + c0, 8)
            total = jnp.sum(b_acc[pl.ds(start, 8), :], axis=1, keepdims=True)
            tile = jnp.where(lane == shift + 50 + part, total, tile)
        sums_ref[pl.ds(at, 8), :] = tile
        return carry

    lax.fori_loop(0, channels // 8, kernel_step, 0)


def back_body(
    g_ref, south_ref, halo_ref, before_ref, after_ref, ct_ref, mask_ref, dw_ref, north_ref,
    out_ref, ext, flat,
):
    rows, channels, cols = g_ref.shape
    pairs = cols // 128
    fill(ext, g_ref, south_ref, halo_ref, before_ref, after_ref)

    def step(ct, carry):
        c0 = pl.multiple_of(ct * 8, 8)
        lane = lanes()
        summed = correlate(
            ext, c0, rows, pairs, lane, dw_ref[pl.ds(c0, 8), :], north_ref[pl.ds(c0, 8), :]
        )
        for i in range(rows):
            for t in range(pairs):
                flat[t, pl.ds(c0 * rows + i, 8, stride=rows), :] = summed[i][t]
        return carry

    lax.fori_loop(0, channels // 8, step, 0)
    sea = mask_ref[...].astype(F32)[None]
    grad = gather(flat, channels, rows) + ct_ref[...].astype(F32) * sea
    out_ref[...] = (grad * sea).astype(BF16)


def lat_halo(first, last):
    n_lat, n_lon = lax.axis_size("lat"), lax.axis_size("lon")
    tops = [i * n_lat + n_lat - 1 for i in range(n_lon)]
    mirror = lax.ppermute(last, ("lon", "lat"), list(zip(tops, tops[::-1])))
    south = lax.ppermute(last, "lat", [(i, i + 1) for i in range(n_lat - 1)])
    north = lax.ppermute(first, "lat", [(i + 1, i) for i in range(n_lat - 1)])
    return south, north, mirror


def lon_halo(left, right):
    n_lon = lax.axis_size("lon")
    before = lax.ppermute(right, "lon", [(i, (i + 1) % n_lon) for i in range(n_lon)])
    after = lax.ppermute(left, "lon", [(i, (i - 1) % n_lon) for i in range(n_lon)])
    return before, after


def like(shape, dtype):
    return jax.ShapeDtypeStruct(shape, dtype)


def halo(rows_of, first, last, flip):
    rows, channels, cols = rows_of.shape
    south, north, mirror = lat_halo(first, last)
    strip = like((channels, 128), BF16)
    fold, left, right = call(
        strips_body, [like((RING, channels, cols), BF16), strip, strip],
        rows_of, south, north, mirror, flip,
    )
    before, after = lon_halo(left, right)
    return south, fold, before, after


def total(sums):
    n_lat, n_lon = lax.axis_size("lat"), lax.axis_size("lon")
    size = sums.shape[0] // n_lat
    pieces = sums.reshape(n_lat, size, 128)
    pieces = lax.all_to_all(pieces, "lat", 0, 0, tiled=True)
    own = jnp.sum(pieces, axis=0, keepdims=True)
    own = lax.all_to_all(jnp.broadcast_to(own, (n_lon, size, 128)), "lon", 0, 0, tiled=True)
    own = jnp.sum(own, axis=0, keepdims=True)
    own = lax.all_to_all(jnp.broadcast_to(own, (n_lat, size, 128)), "lat", 0, 0, tiled=True)
    return own.reshape(n_lat * size, 128)


def shards(fields, land_mask, dw_kernel, gain, w_in, b_in, w_out, cotangent):
    channels, rows, cols = fields.shape
    hidden = w_out.shape[0]
    flip = jnp.eye(cols, dtype=BF16)[::-1]
    taps = dw_kernel.reshape(channels, 49)
    turned = taps[:, ::-1]
    is_top = lax.axis_index("lat") == lax.axis_size("lat") - 1
    north = jnp.where(is_top, taps, turned)
    ring = like((RING, channels, cols), BF16)
    grid = like((rows, channels, cols), BF16)
    whole = like((channels, rows, cols), BF16)
    flat = pltpu.VMEM((cols // 128, channels * rows, 128), F32)
    ext = pltpu.VMEM((rows + 2 * RING, channels, cols + 128), F32)
    masked, first, last = call(rows_body, [grid, ring, ring], fields, land_mask, scratch=[flat])
    south, fold, before, after = halo(masked, first, last, flip)
    cells = rows * cols
    output, grads, first, last, sums = call(
        block_body,
        [whole, grid, ring, ring, like((2 * channels + hidden, 128), F32)],
        masked, south, fold, before, after, cotangent, land_mask,
        taps, gain[:, None], w_in, w_in.T, b_in[:, None], w_out, w_out.T,
        scratch=[
            ext,
            pltpu.VMEM((rows, channels, cols), F32),
            flat,
            pltpu.VMEM((hidden, cells), BF16),
            pltpu.VMEM((channels, cells), BF16),
            pltpu.VMEM((channels, cells), BF16),
            pltpu.VMEM((hidden, cells), BF16),
            pltpu.VMEM((hidden, 128), F32),
            pltpu.VMEM((channels, 128), F32),
        ],
    )
    south, fold, before, after = halo(grads, first, last, flip)
    (input_grad,) = call(
        back_body, [whole], grads, south, fold, before, after, cotangent, land_mask, turned, north,
        scratch=[ext, flat],
    )
    scale = float(cells * lax.axis_size("lat") * lax.axis_size("lon")) ** -0.5
    sums = total(sums) * scale
    low = channels + hidden
    shift = hidden - 128
    tail = sums[low:, shift:]
    return (
        output,
        input_grad,
        tail[:, :49].reshape(channels, 7, 7),
        tail[:, 49],
        jnp.concatenate([sums[:channels], sums[low:, :shift]], axis=1),
        tail[:, 50 : 50 + hidden // channels].T.reshape(hidden),
        sums[channels:low, :channels],
    )


def solution(mesh):
    tiles = P(None, "lat", "lon")
    return jax.shard_map(
        shards,
        mesh=mesh,
        in_specs=(tiles, P("lat", "lon"), P(), P(), P(), P(), P(), tiles),
        out_specs=(tiles, tiles, P(), P(), P(), P(), P()),
        check_vma=False,
    )
```

```python
import functools

import jax
import jax.numpy as jnp
from jax import lax
from jax.experimental import pallas as pl
from jax.experimental.pallas import tpu as pltpu
from jax.sharding import PartitionSpec as P

F32 = jnp.float32
BF16 = jnp.bfloat16
VMEM_LIMIT = 56 * 1024 * 1024
RING = 3


def call(body, outs, *args, scratch=(), smem=0, waits=()):
    specs = [pl.BlockSpec(memory_space=pltpu.VMEM)] * (len(args) - smem)
    specs += [pl.BlockSpec(memory_space=pltpu.SMEM)] * smem
    specs += [pl.BlockSpec(memory_space=pl.ANY)] * len(waits)
    count = len(args)

    def run(*refs):
        body(*refs[:count], *refs[count + len(waits) :])

    return pl.pallas_call(
        run,
        out_shape=outs,
        in_specs=specs,
        out_specs=[pl.BlockSpec(memory_space=pltpu.VMEM)] * len(outs),
        scratch_shapes=list(scratch),
        compiler_params=pltpu.CompilerParams(vmem_limit_bytes=VMEM_LIMIT),
    )(*args, *waits)


def lanes():
    return lax.broadcasted_iota(jnp.int32, (8, 128), 1)


def spread(flat, values):
    channels, rows, cols = values.shape
    for t in range(cols // 128):
        part = values[:, :, t * 128 : t * 128 + 128]
        flat[t] = part.reshape(channels * rows, 128)


def gather(flat, channels, rows):
    parts = [flat[t].reshape(channels, rows, 128) for t in range(flat.shape[0])]
    return jnp.concatenate(parts, axis=2)


def row_of(flat, i, channels, rows):
    parts = [flat[t, pl.ds(i, channels, stride=rows), :] for t in range(flat.shape[0])]
    return jnp.concatenate(parts, axis=1)


def rows_body(f_ref, mask_ref, m_ref, first_ref, last_ref, flat):
    channels, rows, cols = f_ref.shape
    sea = mask_ref[...].astype(F32)
    spread(flat, f_ref[...].astype(F32) * sea[None])
    for i in range(rows):
        row = row_of(flat, i, channels, rows).astype(BF16)
        m_ref[i] = row
        if i < RING:
            first_ref[i] = row
        if i >= rows - RING:
            last_ref[i - (rows - RING)] = row


def strips_body(m_ref, south_ref, north_ref, mirror_ref, halo_ref, left_ref, right_ref):
    rows, channels, cols = m_ref.shape
    here = lax.broadcasted_iota(jnp.int32, (cols, cols), 0)
    there = lax.broadcasted_iota(jnp.int32, (cols, cols), 1)
    flip = (here + there == cols - 1).astype(F32).astype(BF16)
    for k in range(RING):
        turned = jnp.dot(mirror_ref[RING - 1 - k], flip, preferred_element_type=F32)
        halo_ref[k] = (north_ref[k].astype(F32) + turned).astype(BF16)
    lane = lax.broadcasted_iota(jnp.int32, (channels, 128), 1)
    left = jnp.zeros((channels, 128), F32)
    right = jnp.zeros((channels, 128), F32)
    for r in range(rows + 2 * RING):
        if r < RING:
            ref, at = south_ref, r
        elif r < rows + RING:
            ref, at = m_ref, r - RING
        else:
            ref, at = halo_ref, r - RING - rows
        here = (lane >= RING * r) & (lane < RING * r + RING)
        head = ref[at, :, 0:128].astype(F32)
        tail = ref[at, :, cols - 128 : cols].astype(F32)
        if r:
            head = pltpu.roll(head, RING * r, 1)
        tail = pltpu.roll(tail, RING * r + RING, 1)
        left = jnp.where(here, head, left)
        right = jnp.where(here, tail, right)
    left_ref[...] = left.astype(BF16)
    right_ref[...] = right.astype(BF16)


def fill(ext, m_ref, south_ref, halo_ref, before_ref, after_ref):
    rows, channels, cols = m_ref.shape
    lane = lax.broadcasted_iota(jnp.int32, (channels, 128), 1)
    before = before_ref[...].astype(F32)
    after = after_ref[...].astype(F32)
    for r in range(rows + 2 * RING):
        if r < RING:
            row = south_ref[r]
        elif r < rows + RING:
            row = m_ref[r - RING]
        else:
            row = halo_ref[r - RING - rows]
        ext[r, :, 0:cols] = row.astype(F32)
        right = after if r == 0 else pltpu.roll(after, 128 - RING * r, 1)
        left = pltpu.roll(before, 128 - RING - RING * r, 1)
        ext[r, :, cols : cols + 128] = jnp.where(
            lane < RING, right, jnp.where(lane >= 128 - RING, left, 0.0)
        )


def windows(tiles, step, lane):
    if step == 0:
        return tiles[:-1]
    count = len(tiles)
    if step > 0:
        turned = [pltpu.roll(t, 128 - step, 1) for t in tiles]
        keep = lane < 128 - step
        return [jnp.where(keep, turned[t], turned[t + 1]) for t in range(count - 1)]
    turned = [pltpu.roll(t, -step, 1) for t in tiles]
    keep = lane >= -step
    return [jnp.where(keep, turned[t], turned[t - 1]) for t in range(count - 1)]


def tap(weights, index):
    return jnp.broadcast_to(weights[:, index : index + 1], (8, 128))


def correlate(ext, c0, rows, pairs, lane, weights, top):
    summed = [[None] * pairs for _ in range(rows)]
    for b in range(7):
        if top is None:
            taps = [tap(weights, a * 7 + b) for a in range(7)]
            far = taps
        else:
            taps = [tap(weights, 48 - a * 7 - b) for a in range(7)]
            far = [jnp.where(top, tap(weights, a * 7 + b), taps[a]) for a in range(7)]
        for r in range(rows + 2 * RING):
            tiles = [ext[r, pl.ds(c0, 8), t * 128 : t * 128 + 128] for t in range(pairs + 1)]
            wins = windows(tiles, b - RING, lane)
            for a in range(7):
                i = r - a
                if 0 <= i < rows:
                    weight = far[a] if r >= rows + RING else taps[a]
                    for t in range(pairs):
                        term = weight * wins[t]
                        old = summed[i][t]
                        summed[i][t] = term if old is None else old + term
    return summed


def block_body(
    m_ref, south_ref, halo_ref, before_ref, after_ref, ct_ref, mask_ref,
    dw_ref, gain_ref, w_in_ref, b_ref, w_out_ref,
    out_ref, g_ref, first_ref, last_ref, sums_ref,
    ext, conv, flat, act, back, sca, pre, b_acc, gain_acc, tail,
):
    rows, channels, cols = m_ref.shape
    hidden = w_out_ref.shape[0]
    pairs = cols // 128
    fill(ext, m_ref, south_ref, halo_ref, before_ref, after_ref)
    sea = mask_ref[...].astype(F32)
    spread(flat, ct_ref[...].astype(F32) * sea[None])
    for i in range(rows):
        back[:, i * cols : i * cols + cols] = row_of(flat, i, channels, rows).astype(BF16)

    def conv_step(ct, carry):
        c0 = pl.multiple_of(ct * 8, 8)
        lane = lanes()
        summed = correlate(ext, c0, rows, pairs, lane, dw_ref[pl.ds(c0, 8), :], None)
        for i in range(rows):
            for t in range(pairs):
                conv[i, pl.ds(c0, 8), t * 128 : t * 128 + 128] = summed[i][t]
        return carry

    lax.fori_loop(0, channels // 8, conv_step, 0)

    b_acc[...] = jnp.zeros_like(b_acc)
    gain_acc[...] = jnp.zeros_like(gain_acc)
    gain = jnp.broadcast_to(gain_ref[...], (128, channels)).T
    gain = jnp.concatenate([gain] * pairs, axis=1)
    bias = jnp.broadcast_to(b_ref[...], (128, hidden)).T
    bias = jnp.concatenate([bias] * pairs, axis=1)
    w_in_t = w_in_ref[...].T
    w_out_t = w_out_ref[...].T
    root = 0.7978845608028654
    for i in range(rows):
        span = slice(i * cols, i * cols + cols)
        raw = conv[i]
        centred = raw - jnp.mean(raw, axis=0, keepdims=True)
        inv_std = lax.rsqrt(jnp.mean(centred * centred, axis=0, keepdims=True) + 1e-06)
        normed = centred * inv_std
        scaled = (normed * gain).astype(BF16)
        sca[:, span] = scaled
        v = jnp.dot(w_in_t, scaled, preferred_element_type=F32) + bias
        v2 = v * v
        t = jnp.tanh(root * v * (1.0 + 0.044715 * v2))
        half = 0.5 * (1.0 + t)
        activated = (v * half).astype(BF16)
        act[:, span] = activated
        slope = half + 0.5 * v * (1.0 - t * t) * (root * (1.0 + 3 * 0.044715 * v2))
        mixed = jnp.dot(w_out_t, activated, preferred_element_type=F32)
        mixed = m_ref[i].astype(F32) + mixed
        for t in range(pairs):
            flat[t, pl.ds(i, channels, stride=rows), :] = mixed[:, t * 128 : t * 128 + 128]
        act_grad = jnp.dot(w_out_ref[...], back[:, span], preferred_element_type=F32)
        pre_grad = (act_grad * slope).astype(BF16)
        pre[:, span] = pre_grad
        wide = pre_grad.astype(F32)
        b_acc[...] += sum(wide[:, t * 128 : t * 128 + 128] for t in range(pairs))
        scaled_grad = jnp.dot(w_in_ref[...], pre_grad, preferred_element_type=F32)
        gains = scaled_grad * normed
        gain_acc[...] += sum(gains[:, t * 128 : t * 128 + 128] for t in range(pairs))
        norm_grad = scaled_grad * gain
        grad = inv_std * (
            norm_grad
            - jnp.mean(norm_grad, axis=0, keepdims=True)
            - normed * jnp.mean(norm_grad * normed, axis=0, keepdims=True)
        )
        conv[i] = grad
        short = grad.astype(BF16)
        g_ref[i] = short
        if i < RING:
            first_ref[i] = short
        if i >= rows - RING:
            last_ref[i - (rows - RING)] = short

    out_ref[...] = (gather(flat, channels, rows) * sea[None]).astype(BF16)
    over_cells = (((1,), (1,)), ((), ()))
    w_in_sum = lax.dot_general(sca[...], pre[...], over_cells, preferred_element_type=F32)
    w_out_sum = lax.dot_general(act[...], back[...], over_cells, preferred_element_type=F32)
    low = channels + hidden
    shift = hidden - 128
    sums_ref[0:channels, :] = w_in_sum[:, 0:128].astype(BF16)
    blank = jnp.zeros((hidden, 128 - channels), F32)
    sums_ref[channels:low, :] = jnp.concatenate([w_out_sum, blank], axis=1).astype(BF16)
    blank = jnp.zeros((channels, 128 - shift), F32)
    tail[...] = jnp.concatenate([w_in_sum[:, 128:hidden], blank], axis=1)

    def kernel_step(ct, carry):
        c0 = pl.multiple_of(ct * 8, 8)
        lane = lanes()
        tile = tail[pl.ds(c0, 8), :]
        grads = [
            [conv[i, pl.ds(c0, 8), t * 128 : t * 128 + 128] for t in range(pairs)]
            for i in range(rows)
        ]
        for b in range(7):
            summed = [None] * 7
            for r in range(rows + 2 * RING):
                tiles = [ext[r, pl.ds(c0, 8), t * 128 : t * 128 + 128] for t in range(pairs + 1)]
                wins = windows(tiles, b - RING, lane)
                for a in range(7):
                    i = r - a
                    if 0 <= i < rows:
                        for t in range(pairs):
                            term = grads[i][t] * wins[t]
                            summed[a] = term if summed[a] is None else summed[a] + term
            for a in range(7):
                total = jnp.sum(summed[a], axis=1, keepdims=True)
                tile = jnp.where(lane == shift + a * 7 + b, total, tile)
        total = jnp.sum(gain_acc[pl.ds(c0, 8), :], axis=1, keepdims=True)
        tile = jnp.where(lane == shift + 49, total, tile)
        for part in range(hidden // channels):
            start = pl.multiple_of(part * channels + c0, 8)
            total = jnp.sum(b_acc[pl.ds(start, 8), :], axis=1, keepdims=True)
            tile = jnp.where(lane == shift + 50 + part, total, tile)
        tail[pl.ds(c0, 8), :] = tile
        return carry

    lax.fori_loop(0, channels // 8, kernel_step, 0)
    sums_ref[low : low + channels, :] = tail[...].astype(BF16)


def back_body(
    g_ref, south_ref, halo_ref, before_ref, after_ref, ct_ref, mask_ref, dw_ref, top_ref,
    out_ref, ext, flat,
):
    rows, channels, cols = g_ref.shape
    pairs = cols // 128
    fill(ext, g_ref, south_ref, halo_ref, before_ref, after_ref)

    def step(ct, carry):
        c0 = pl.multiple_of(ct * 8, 8)
        lane = lanes()
        top = jnp.broadcast_to(top_ref[0], (8, 128)) > 0
        summed = correlate(ext, c0, rows, pairs, lane, dw_ref[pl.ds(c0, 8), :], top)
        for i in range(rows):
            for t in range(pairs):
                flat[t, pl.ds(c0 * rows + i, 8, stride=rows), :] = summed[i][t]
        return carry

    lax.fori_loop(0, channels // 8, step, 0)
    sea = mask_ref[...].astype(F32)[None]
    grad = gather(flat, channels, rows) + ct_ref[...].astype(F32) * sea
    out_ref[...] = (grad * sea).astype(BF16)


def lat_halo(first, last):
    n_lat, n_lon = lax.axis_size("lat"), lax.axis_size("lon")
    tops = [i * n_lat + n_lat - 1 for i in range(n_lon)]
    mirror = lax.ppermute(last, ("lon", "lat"), list(zip(tops, tops[::-1])))
    south = lax.ppermute(last, "lat", [(i, i + 1) for i in range(n_lat - 1)])
    north = lax.ppermute(first, "lat", [(i + 1, i) for i in range(n_lat - 1)])
    return south, north, mirror


def lon_halo(left, right):
    n_lon = lax.axis_size("lon")
    before = lax.ppermute(right, "lon", [(i, (i + 1) % n_lon) for i in range(n_lon)])
    after = lax.ppermute(left, "lon", [(i, (i - 1) % n_lon) for i in range(n_lon)])
    return before, after


def like(shape, dtype):
    return jax.ShapeDtypeStruct(shape, dtype)


def halo(rows_of, first, last):
    rows, channels, cols = rows_of.shape
    south, north, mirror = lat_halo(first, last)
    strip = like((channels, 128), BF16)
    fold, left, right = call(
        strips_body, [like((RING, channels, cols), BF16), strip, strip],
        rows_of, south, north, mirror,
    )
    before, after = lon_halo(left, right)
    return (south, fold, before, after), left


def spread_body(pieces_ref, out_ref):
    summed = jnp.sum(pieces_ref[...].astype(F32), axis=0).astype(out_ref.dtype)
    for i in range(out_ref.shape[0]):
        out_ref[i] = summed


def unpack_body(scale, sums_ref, w_in_ref, w_out_ref, dw_ref, gain_ref, b_ref):
    channels, hidden = w_in_ref.shape
    low = channels + hidden
    shift = hidden - 128
    tail = sums_ref[low : low + channels, :] * scale
    w_in_ref[...] = jnp.concatenate([sums_ref[0:channels, :] * scale, tail[:, 0:shift]], axis=1)
    w_out_ref[...] = sums_ref[channels:low, 0:channels] * scale
    dw_ref[...] = tail[:, shift : shift + 49]
    turned = tail.T
    gain_ref[...] = turned[shift + 49 : shift + 50, :]
    parts = [turned[shift + 50 + k : shift + 51 + k, :] for k in range(hidden // channels)]
    b_ref[...] = jnp.concatenate(parts, axis=1)


def shards(fields, land_mask, dw_kernel, gain, w_in, b_in, w_out, cotangent):
    channels, rows, cols = fields.shape
    hidden = w_out.shape[0]
    n_lat, n_lon = lax.axis_size("lat"), lax.axis_size("lon")
    taps = dw_kernel.reshape(channels, 49)
    is_top = (lax.axis_index("lat") == n_lat - 1).astype(jnp.int32).reshape(1)
    ring = like((RING, channels, cols), BF16)
    grid = like((rows, channels, cols), BF16)
    whole = like((channels, rows, cols), BF16)
    flat = pltpu.VMEM((cols // 128, channels * rows, 128), F32)
    ext = pltpu.VMEM((rows + 2 * RING, channels, cols + 128), F32)
    masked, first, last = call(rows_body, [grid, ring, ring], fields, land_mask, scratch=[flat])
    around, _ = halo(masked, first, last)
    cells = rows * cols
    height = 2 * channels + hidden
    output, grads, first, last, sums = call(
        block_body,
        [whole, grid, ring, ring, like((height, 128), BF16)],
        masked, *around, cotangent, land_mask,
        taps, gain.reshape(1, channels), w_in, b_in.reshape(1, hidden), w_out,
        scratch=[
            ext,
            pltpu.VMEM((rows, channels, cols), F32),
            flat,
            pltpu.VMEM((hidden, cells), BF16),
            pltpu.VMEM((channels, cells), BF16),
            pltpu.VMEM((channels, cells), BF16),
            pltpu.VMEM((hidden, cells), BF16),
            pltpu.VMEM((hidden, 128), F32),
            pltpu.VMEM((channels, 128), F32),
            pltpu.VMEM((channels, 128), F32),
        ],
    )
    size = height // n_lat
    around, strip = halo(grads, first, last)
    pieces = lax.all_to_all(sums.reshape(n_lat, size, 128), "lat", 0, 0, tiled=True)
    (pieces,) = call(spread_body, [like((n_lon, size, 128), BF16)], pieces, waits=[strip])
    pieces = lax.all_to_all(pieces, "lon", 0, 0, tiled=True)
    (pieces,) = call(spread_body, [like((n_lat, size, 128), F32)], pieces, waits=around[2:])
    pieces = lax.all_to_all(pieces, "lat", 0, 0, tiled=True)
    (input_grad,) = call(
        back_body, [whole], grads, *around, cotangent, land_mask, taps, is_top,
        scratch=[ext, flat], smem=1,
    )
    scale = float(cells * n_lat * n_lon) ** -0.5
    w_in_grad, w_out_grad, dw_grad, gain_grad, b_grad = call(
        functools.partial(unpack_body, scale),
        [
            like((channels, hidden), F32),
            like((hidden, channels), F32),
            like((channels, 49), F32),
            like((1, channels), F32),
            like((1, hidden), F32),
        ],
        pieces.reshape(height, 128),
    )
    return (
        output,
        input_grad,
        dw_grad.reshape(channels, 7, 7),
        gain_grad.reshape(channels),
        w_in_grad,
        b_grad.reshape(hidden),
        w_out_grad,
    )


def solution(mesh):
    tiles = P(None, "lat", "lon")
    return jax.shard_map(
        shards,
        mesh=mesh,
        in_specs=(tiles, P("lat", "lon"), P(), P(), P(), P(), P(), tiles),
        out_specs=(tiles, tiles, P(), P(), P(), P(), P()),
        check_vma=False,
    )
```

```python
import functools

import jax
import jax.numpy as jnp
from jax import lax
from jax.experimental import pallas as pl
from jax.experimental.pallas import tpu as pltpu
from jax.sharding import PartitionSpec as P

F32 = jnp.float32
BF16 = jnp.bfloat16
VMEM_LIMIT = 48 * 1024 * 1024
RING = 3


def call(body, outs, args, raw=(), scalars=(), scratch=(), waits=()):
    count = len(args)
    end = count + len(raw) + len(scalars) + len(waits)
    specs = [pl.BlockSpec(memory_space=pltpu.VMEM)] * count
    specs += [pl.BlockSpec(memory_space=pltpu.HBM)] * len(raw)
    specs += [pl.BlockSpec(memory_space=pltpu.SMEM)] * len(scalars)
    specs += [pl.BlockSpec(memory_space=pl.ANY)] * len(waits)
    near = [pltpu.with_memory_space_constraint(x, pltpu.VMEM) for x in args]
    far = [pltpu.with_memory_space_constraint(x, pltpu.HBM) for x in raw]
    slots = [pltpu.VMEM(x.shape, x.dtype) for x in raw]

    def run(*refs):
        first = end + len(outs)
        made = refs[len(refs) - 1 - len(raw) : len(refs) - 1] if raw else ()
        inner = refs[first : len(refs) - 1 - len(raw)] if raw else refs[first:]
        rest = (*refs[count + len(raw) : end - len(waits)], *refs[end:first], *inner)
        if not raw:
            return body(*refs[:count], *rest)
        copies = [
            pltpu.make_async_copy(refs[count + i], made[i], refs[-1].at[i])
            for i in range(len(raw))
        ]
        for copy in copies:
            copy.start()

        def settle():
            for copy in copies:
                copy.wait()

        return body(settle, *refs[:count], *made, *rest)

    extra = [*slots, pltpu.SemaphoreType.DMA((len(raw),))] if raw else []
    return pl.pallas_call(
        run,
        out_shape=outs,
        in_specs=specs,
        out_specs=[pl.BlockSpec(memory_space=pltpu.VMEM)] * len(outs),
        scratch_shapes=[*scratch, *extra],
        compiler_params=pltpu.CompilerParams(vmem_limit_bytes=VMEM_LIMIT),
    )(*near, *far, *scalars, *waits)


def lanes():
    return lax.broadcasted_iota(jnp.int32, (8, 128), 1)


def spread(flat, values):
    channels, rows, cols = values.shape
    for t in range(cols // 128):
        part = values[:, :, t * 128 : t * 128 + 128]
        flat[t] = part.reshape(channels * rows, 128)


def gather(flat, channels, rows):
    parts = [flat[t].reshape(channels, rows, 128) for t in range(flat.shape[0])]
    return jnp.concatenate(parts, axis=2)


def row_of(flat, i, channels, rows):
    parts = [flat[t, pl.ds(i, channels, stride=rows), :] for t in range(flat.shape[0])]
    return jnp.concatenate(parts, axis=1)


def rows_body(settle, f_ref, mask_ref, m_ref, first_ref, last_ref, flat):
    channels, rows, cols = f_ref.shape
    settle()
    spread(flat, f_ref[...].astype(F32) * mask_ref[...].astype(F32)[None])
    for i in range(rows):
        row = row_of(flat, i, channels, rows).astype(BF16)
        m_ref[i] = row
        if i < RING:
            first_ref[i] = row
        if i >= rows - RING:
            last_ref[i - (rows - RING)] = row


def turn_body(mirror_ref, turned_ref):
    cols = mirror_ref.shape[2]
    here = lax.broadcasted_iota(jnp.int32, (cols, cols), 0)
    there = lax.broadcasted_iota(jnp.int32, (cols, cols), 1)
    flip = (here + there == cols - 1).astype(F32).astype(BF16)
    for k in range(RING):
        row = jnp.dot(mirror_ref[RING - 1 - k], flip, preferred_element_type=F32)
        turned_ref[k] = row.astype(BF16)


def strips_body(m_ref, south_ref, north_ref, turned_ref, halo_ref, left_ref, right_ref):
    rows, channels, cols = m_ref.shape
    for k in range(RING):
        halo_ref[k] = (north_ref[k].astype(F32) + turned_ref[k].astype(F32)).astype(BF16)
    lane = lax.broadcasted_iota(jnp.int32, (channels, 128), 1)
    left = jnp.zeros((channels, 128), F32)
    right = jnp.zeros((channels, 128), F32)
    for r in range(rows + 2 * RING):
        if r < RING:
            ref, at = south_ref, r
        elif r < rows + RING:
            ref, at = m_ref, r - RING
        else:
            ref, at = halo_ref, r - RING - rows
        here = (lane >= RING * r) & (lane < RING * r + RING)
        head = ref[at, :, 0:128].astype(F32)
        tail = ref[at, :, cols - 128 : cols].astype(F32)
        if r:
            head = pltpu.roll(head, RING * r, 1)
        tail = pltpu.roll(tail, RING * r + RING, 1)
        left = jnp.where(here, head, left)
        right = jnp.where(here, tail, right)
    left_ref[...] = left.astype(BF16)
    right_ref[...] = right.astype(BF16)


def strips_and_sums_body(
    m_ref, south_ref, north_ref, turned_ref, sums_ref, halo_ref, left_ref, right_ref, out_ref
):
    strips_body(m_ref, south_ref, north_ref, turned_ref, halo_ref, left_ref, right_ref)
    out_ref[...] = sums_ref[...]


def fill(ext, m_ref, south_ref, halo_ref, before_ref, after_ref):
    rows, channels, cols = m_ref.shape
    lane = lax.broadcasted_iota(jnp.int32, (channels, 128), 1)
    before = before_ref[...].astype(F32)
    after = after_ref[...].astype(F32)
    for r in range(rows + 2 * RING):
        if r < RING:
            row = south_ref[r]
        elif r < rows + RING:
            row = m_ref[r - RING]
        else:
            row = halo_ref[r - RING - rows]
        ext[r, :, 0:cols] = row.astype(F32)
        right = after if r == 0 else pltpu.roll(after, 128 - RING * r, 1)
        left = pltpu.roll(before, 128 - RING - RING * r, 1)
        ext[r, :, cols : cols + 128] = jnp.where(
            lane < RING, right, jnp.where(lane >= 128 - RING, left, 0.0)
        )


def windows(tiles, step, lane):
    if step == 0:
        return tiles[:-1]
    count = len(tiles)
    if step > 0:
        turned = [pltpu.roll(t, 128 - step, 1) for t in tiles]
        keep = lane < 128 - step
        return [jnp.where(keep, turned[t], turned[t + 1]) for t in range(count - 1)]
    turned = [pltpu.roll(t, -step, 1) for t in tiles]
    keep = lane >= -step
    return [jnp.where(keep, turned[t], turned[t - 1]) for t in range(count - 1)]


def tap_columns(dw_ref):
    rows = jnp.concatenate([dw_ref[a] for a in range(7)], axis=0)
    blank = jnp.zeros((128 - rows.shape[0], rows.shape[1]), F32)
    return jnp.concatenate([rows, blank], axis=0).T


def tap(weights, index):
    return jnp.broadcast_to(weights[:, index : index + 1], (8, 128))


def correlate(ext, c0, rows, pairs, lane, weights, top):
    summed = [[None] * pairs for _ in range(rows)]
    for b in range(7):
        if top is None:
            taps = [tap(weights, a * 7 + b) for a in range(7)]
            far = taps
        else:
            taps = [tap(weights, 48 - a * 7 - b) for a in range(7)]
            far = [jnp.where(top, tap(weights, a * 7 + b), taps[a]) for a in range(7)]
        for r in range(rows + 2 * RING):
            tiles = [ext[r, pl.ds(c0, 8), t * 128 : t * 128 + 128] for t in range(pairs + 1)]
            wins = windows(tiles, b - RING, lane)
            for a in range(7):
                i = r - a
                if 0 <= i < rows:
                    weight = far[a] if r >= rows + RING else taps[a]
                    for t in range(pairs):
                        term = weight * wins[t]
                        old = summed[i][t]
                        summed[i][t] = term if old is None else old + term
    return summed


def block_body(
    settle, m_ref, south_ref, halo_ref, before_ref, after_ref, ct_ref, mask_ref,
    dw_ref, gain_ref, w_in_ref, b_ref, w_out_ref,
    out_ref, g_ref, first_ref, last_ref, wide_ref, tail_ref, ext_ref,
    conv, flat, act, back, sca, pre, b_acc, gain_acc, taps,
):
    ext = ext_ref
    rows, channels, cols = m_ref.shape
    hidden = w_out_ref.shape[0]
    pairs = cols // 128
    fill(ext, m_ref, south_ref, halo_ref, before_ref, after_ref)
    settle()
    taps[...] = tap_columns(dw_ref)
    sea = mask_ref[...].astype(F32)
    spread(flat, ct_ref[...].astype(F32) * sea[None])
    for i in range(rows):
        back[:, i * cols : i * cols + cols] = row_of(flat, i, channels, rows).astype(BF16)

    def conv_step(ct, carry):
        c0 = pl.multiple_of(ct * 8, 8)
        lane = lanes()
        summed = correlate(ext, c0, rows, pairs, lane, taps[pl.ds(c0, 8), :], None)
        for i in range(rows):
            for t in range(pairs):
                conv[i, pl.ds(c0, 8), t * 128 : t * 128 + 128] = summed[i][t]
        return carry

    lax.fori_loop(0, channels // 8, conv_step, 0)

    b_acc[...] = jnp.zeros_like(b_acc)
    gain_acc[...] = jnp.zeros_like(gain_acc)
    gain = jnp.broadcast_to(gain_ref[...], (128, channels)).T
    gain = jnp.concatenate([gain] * pairs, axis=1)
    bias = jnp.broadcast_to(b_ref[...], (128, hidden)).T
    bias = jnp.concatenate([bias] * pairs, axis=1)
    w_in_t = w_in_ref[...].T
    w_out_t = w_out_ref[...].T
    root = 0.7978845608028654
    for i in range(rows):
        span = slice(i * cols, i * cols + cols)
        raw = conv[i]
        centred = raw - jnp.mean(raw, axis=0, keepdims=True)
        inv_std = lax.rsqrt(jnp.mean(centred * centred, axis=0, keepdims=True) + 1e-06)
        normed = centred * inv_std
        scaled = (normed * gain).astype(BF16)
        sca[:, span] = scaled
        v = jnp.dot(w_in_t, scaled, preferred_element_type=F32) + bias
        v2 = v * v
        t = jnp.tanh(root * v * (1.0 + 0.044715 * v2))
        half = 0.5 * (1.0 + t)
        activated = (v * half).astype(BF16)
        act[:, span] = activated
        slope = half + 0.5 * v * (1.0 - t * t) * (root * (1.0 + 3 * 0.044715 * v2))
        mixed = jnp.dot(w_out_t, activated, preferred_element_type=F32)
        mixed = m_ref[i].astype(F32) + mixed
        for t in range(pairs):
            flat[t, pl.ds(i, channels, stride=rows), :] = mixed[:, t * 128 : t * 128 + 128]
        act_grad = jnp.dot(w_out_ref[...], back[:, span], preferred_element_type=F32)
        pre_grad = (act_grad * slope).astype(BF16)
        pre[:, span] = pre_grad
        wide = pre_grad.astype(F32)
        b_acc[...] += sum(wide[:, t * 128 : t * 128 + 128] for t in range(pairs))
        scaled_grad = jnp.dot(w_in_ref[...], pre_grad, preferred_element_type=F32)
        gains = scaled_grad * normed
        gain_acc[...] += sum(gains[:, t * 128 : t * 128 + 128] for t in range(pairs))
        norm_grad = scaled_grad * gain
        grad = inv_std * (
            norm_grad
            - jnp.mean(norm_grad, axis=0, keepdims=True)
            - normed * jnp.mean(norm_grad * normed, axis=0, keepdims=True)
        )
        short = grad.astype(BF16)
        g_ref[i] = short
        if i < RING:
            first_ref[i] = short
        if i >= rows - RING:
            last_ref[i - (rows - RING)] = short

    out_ref[...] = (gather(flat, channels, rows) * sea[None]).astype(BF16)
    over_cells = (((1,), (1,)), ((), ()))
    w_in_sum = lax.dot_general(sca[...], pre[...], over_cells, preferred_element_type=F32)
    w_out_sum = lax.dot_general(act[...], back[...], over_cells, preferred_element_type=F32)
    low = channels + hidden
    shift = hidden - 128
    wide_ref[0:channels, :] = w_in_sum[:, 0:128].astype(BF16)
    blank = jnp.zeros((hidden, 128 - channels), F32)
    wide_ref[channels:low, :] = jnp.concatenate([w_out_sum, blank], axis=1).astype(BF16)
    blank = jnp.zeros((channels, 128 - shift), F32)
    tail = jnp.concatenate([w_in_sum[:, 128:hidden], blank], axis=1)
    lane = lax.broadcasted_iota(jnp.int32, (channels, 128), 1)
    tail = jnp.where(lane == shift + 49, jnp.sum(gain_acc[...], axis=1, keepdims=True), tail)
    for part in range(hidden // channels):
        column = jnp.sum(b_acc[part * channels : part * channels + channels, :], axis=1, keepdims=True)
        tail = jnp.where(lane == shift + 50 + part, column, tail)
    tail_ref[...] = tail


def kernel_body(shift, ext, g_ref, wide_ref, tail_ref, sums_ref, tail, grid):
    rows, channels, cols = g_ref.shape
    pairs = cols // 128
    grid[...] = g_ref[...].astype(F32)

    def kernel_step(ct, carry):
        c0 = pl.multiple_of(ct * 8, 8)
        lane = lanes()
        tile = tail_ref[pl.ds(c0, 8), :]
        grads = [
            [grid[i, pl.ds(c0, 8), t * 128 : t * 128 + 128] for t in range(pairs)]
            for i in range(rows)
        ]
        for b in range(7):
            summed = [None] * 7
            for r in range(rows + 2 * RING):
                tiles = [ext[r, pl.ds(c0, 8), t * 128 : t * 128 + 128] for t in range(pairs + 1)]
                wins = windows(tiles, b - RING, lane)
                for a in range(7):
                    i = r - a
                    if 0 <= i < rows:
                        for t in range(pairs):
                            term = grads[i][t] * wins[t]
                            summed[a] = term if summed[a] is None else summed[a] + term
            for a in range(7):
                total = jnp.sum(summed[a], axis=1, keepdims=True)
                tile = jnp.where(lane == shift + a * 7 + b, total, tile)
        tail[pl.ds(c0, 8), :] = tile
        return carry

    lax.fori_loop(0, channels // 8, kernel_step, 0)
    low = wide_ref.shape[0]
    sums_ref[0:low, :] = wide_ref[...]
    sums_ref[low : low + channels, :] = tail[...].astype(BF16)


def back_body(
    settle, g_ref, south_ref, halo_ref, before_ref, after_ref, ct_ref, mask_ref, dw_ref, top_ref,
    out_ref, ext, flat, taps,
):
    rows, channels, cols = g_ref.shape
    pairs = cols // 128
    fill(ext, g_ref, south_ref, halo_ref, before_ref, after_ref)
    settle()
    taps[...] = tap_columns(dw_ref)

    def step(ct, carry):
        c0 = pl.multiple_of(ct * 8, 8)
        lane = lanes()
        top = jnp.broadcast_to(top_ref[0], (8, 128)) > 0
        summed = correlate(ext, c0, rows, pairs, lane, taps[pl.ds(c0, 8), :], top)
        for i in range(rows):
            for t in range(pairs):
                flat[t, pl.ds(c0 * rows + i, 8, stride=rows), :] = summed[i][t]
        return carry

    lax.fori_loop(0, channels // 8, step, 0)
    sea = mask_ref[...].astype(F32)[None]
    grad = gather(flat, channels, rows) + ct_ref[...].astype(F32) * sea
    out_ref[...] = (grad * sea).astype(BF16)


def lat_halo(first, last):
    n_lat, n_lon = lax.axis_size("lat"), lax.axis_size("lon")
    tops = [i * n_lat + n_lat - 1 for i in range(n_lon)]
    mirror = lax.ppermute(last, ("lon", "lat"), list(zip(tops, tops[::-1])))
    south = lax.ppermute(last, "lat", [(i, i + 1) for i in range(n_lat - 1)])
    north = lax.ppermute(first, "lat", [(i + 1, i) for i in range(n_lat - 1)])
    (turned,) = call(turn_body, [pltpu.VMEM(last.shape, last.dtype)], [mirror])
    return south, north, turned


def lon_halo(left, right):
    n_lon = lax.axis_size("lon")
    before = lax.ppermute(right, "lon", [(i, (i + 1) % n_lon) for i in range(n_lon)])
    after = lax.ppermute(left, "lon", [(i, (i - 1) % n_lon) for i in range(n_lon)])
    return before, after


def held(struct):
    return pltpu.VMEM(struct.shape, struct.dtype)


def like(shape, dtype):
    return jax.ShapeDtypeStruct(shape, dtype)


def spread_body(pieces_ref, out_ref):
    summed = jnp.sum(pieces_ref[...].astype(F32), axis=0).astype(out_ref.dtype)
    for i in range(out_ref.shape[0]):
        out_ref[i] = summed


def unpack_body(scale, sums_ref, w_in_ref, w_out_ref, dw_ref, gain_ref, b_ref):
    channels, hidden = w_in_ref.shape
    low = channels + hidden
    shift = hidden - 128
    tail = sums_ref[low : low + channels, :] * scale
    w_in_ref[...] = jnp.concatenate([sums_ref[0:channels, :] * scale, tail[:, 0:shift]], axis=1)
    w_out_ref[...] = sums_ref[channels:low, 0:channels] * scale
    turned = tail.T
    for a in range(7):
        dw_ref[a] = turned[shift + 7 * a : shift + 7 * a + 7, :]
    gain_ref[...] = turned[shift + 49 : shift + 50, :]
    parts = [turned[shift + 50 + k : shift + 51 + k, :] for k in range(hidden // channels)]
    b_ref[...] = jnp.concatenate(parts, axis=1)


def shards(fields, land_mask, dw_kernel, gain, w_in, b_in, w_out, cotangent):
    channels, rows, cols = fields.shape
    hidden = w_out.shape[0]
    n_lat, n_lon = lax.axis_size("lat"), lax.axis_size("lon")
    taps = dw_kernel.transpose(1, 2, 0)
    is_top = (lax.axis_index("lat") == n_lat - 1).astype(jnp.int32).reshape(1)
    ring = like((RING, channels, cols), BF16)
    grid = like((rows, channels, cols), BF16)
    whole = like((channels, rows, cols), BF16)
    flat = pltpu.VMEM((cols // 128, channels * rows, 128), F32)
    ext = pltpu.VMEM((rows + 2 * RING, channels, cols + 128), F32)
    near_ring = held(ring)
    strip = pltpu.VMEM((channels, 128), BF16)
    height = 2 * channels + hidden
    near_sums = pltpu.VMEM((height, 128), BF16)
    cells = rows * cols
    masked, first, last = call(
        rows_body, [held(grid), near_ring, near_ring], [], [fields, land_mask], scratch=[flat]
    )
    south, north, turned = lat_halo(first, last)
    fold, left, right = call(
        strips_body, [near_ring, strip, strip], [masked, south, north, turned]
    )
    before, after = lon_halo(left, right)
    columns = pltpu.VMEM((channels, 128), F32)
    output, grads, first, last, wide, tail, ext_rows = call(
        block_body,
        [
            whole, held(grid), near_ring, near_ring,
            pltpu.VMEM((height - channels, 128), BF16), columns, ext,
        ],
        [masked, south, fold, before, after],
        [
            cotangent, land_mask, taps, gain.reshape(1, channels), w_in,
            b_in.reshape(1, hidden), w_out,
        ],
        scratch=[
            pltpu.VMEM((rows, channels, cols), F32),
            flat,
            pltpu.VMEM((hidden, cells), BF16),
            pltpu.VMEM((channels, cells), BF16),
            pltpu.VMEM((channels, cells), BF16),
            pltpu.VMEM((hidden, cells), BF16),
            pltpu.VMEM((hidden, 128), F32),
            columns,
            columns,
        ],
    )
    south, north, turned = lat_halo(first, last)
    (sums,) = call(
        functools.partial(kernel_body, hidden - 128), [near_sums], [ext_rows, grads, wide, tail],
        scratch=[columns, pltpu.VMEM((rows, channels, cols), F32)],
    )
    fold, left, right, sums = call(
        strips_and_sums_body, [near_ring, strip, strip, near_sums],
        [grads, south, north, turned, sums],
    )
    before, after = lon_halo(left, right)
    size = height // n_lat
    pieces = lax.all_to_all(sums.reshape(n_lat, size, 128), "lat", 0, 0, tiled=True)
    (pieces,) = call(
        spread_body, [pltpu.VMEM((n_lon, size, 128), BF16)], [pieces], waits=[before, after]
    )
    pieces = lax.all_to_all(pieces, "lon", 0, 0, tiled=True)
    (pieces,) = call(spread_body, [pltpu.VMEM((n_lat, size, 128), F32)], [pieces])
    pieces = lax.all_to_all(pieces, "lat", 0, 0, tiled=True)
    (input_grad,) = call(
        back_body, [whole], [grads, south, fold, before, after], [cotangent, land_mask, taps],
        [is_top], scratch=[ext, flat, columns],
    )
    scale = float(cells * n_lat * n_lon) ** -0.5
    w_in_grad, w_out_grad, dw_grad, gain_grad, b_grad = call(
        functools.partial(unpack_body, scale),
        [
            like((channels, hidden), F32),
            like((hidden, channels), F32),
            like((7, 7, channels), F32),
            like((1, channels), F32),
            like((1, hidden), F32),
        ],
        [pieces.reshape(height, 128)],
    )
    return (
        output,
        input_grad,
        dw_grad.transpose(2, 0, 1),
        gain_grad.reshape(channels),
        w_in_grad,
        b_grad.reshape(hidden),
        w_out_grad,
    )


def solution(mesh):
    tiles = P(None, "lat", "lon")
    return jax.shard_map(
        shards,
        mesh=mesh,
        in_specs=(tiles, P("lat", "lon"), P(), P(), P(), P(), P(), tiles),
        out_specs=(tiles, tiles, P(), P(), P(), P(), P()),
        check_vma=False,
    )
```

```python
import functools

import jax
import jax.numpy as jnp
from jax import lax
from jax.experimental import pallas as pl
from jax.experimental.pallas import tpu as pltpu
from jax.sharding import PartitionSpec as P

F32 = jnp.float32
BF16 = jnp.bfloat16
VMEM_LIMIT = 48 * 1024 * 1024
RING = 3


def call(body, outs, args, raw=(), scalars=(), scratch=(), waits=()):
    count = len(args)
    end = count + len(raw) + len(scalars) + len(waits)
    specs = [pl.BlockSpec(memory_space=pltpu.VMEM)] * count
    specs += [pl.BlockSpec(memory_space=pltpu.HBM)] * len(raw)
    specs += [pl.BlockSpec(memory_space=pltpu.SMEM)] * len(scalars)
    specs += [pl.BlockSpec(memory_space=pl.ANY)] * len(waits)
    near = [pltpu.with_memory_space_constraint(x, pltpu.VMEM) for x in args]
    far = [pltpu.with_memory_space_constraint(x, pltpu.HBM) for x in raw]
    slots = [pltpu.VMEM(x.shape, x.dtype) for x in raw]

    def run(*refs):
        first = end + len(outs)
        made = refs[len(refs) - 1 - len(raw) : len(refs) - 1] if raw else ()
        inner = refs[first : len(refs) - 1 - len(raw)] if raw else refs[first:]
        rest = (*refs[count + len(raw) : end - len(waits)], *refs[end:first], *inner)
        if not raw:
            return body(*refs[:count], *rest)
        copies = [
            pltpu.make_async_copy(refs[count + i], made[i], refs[-1].at[i])
            for i in range(len(raw))
        ]
        for copy in copies:
            copy.start()

        def settle():
            for copy in copies:
                copy.wait()

        return body(settle, *refs[:count], *made, *rest)

    extra = [*slots, pltpu.SemaphoreType.DMA((len(raw),))] if raw else []
    return pl.pallas_call(
        run,
        out_shape=outs,
        in_specs=specs,
        out_specs=[pl.BlockSpec(memory_space=pltpu.VMEM)] * len(outs),
        scratch_shapes=[*scratch, *extra],
        compiler_params=pltpu.CompilerParams(vmem_limit_bytes=VMEM_LIMIT),
    )(*near, *far, *scalars, *waits)


def lanes():
    return lax.broadcasted_iota(jnp.int32, (8, 128), 1)


def spread(flat, values):
    channels, rows, cols = values.shape
    for t in range(cols // 128):
        part = values[:, :, t * 128 : t * 128 + 128]
        flat[t] = part.reshape(channels * rows, 128)


def gather(flat, channels, rows):
    parts = [flat[t].reshape(channels, rows, 128) for t in range(flat.shape[0])]
    return jnp.concatenate(parts, axis=2)


def row_of(flat, i, channels, rows):
    parts = [flat[t, pl.ds(i, channels, stride=rows), :] for t in range(flat.shape[0])]
    return jnp.concatenate(parts, axis=1)


def choose(flag, yes, no):
    return jnp.where(jnp.broadcast_to(flag, yes.shape) > 0, yes, no)


def rows_body(settle, f_ref, mask_ref, place_ref, m_ref, inner_ref, outer_ref, flat):
    channels, rows, cols = f_ref.shape
    settle()
    spread(flat, f_ref[...].astype(F32) * mask_ref[...].astype(F32)[None])
    kept = [row_of(flat, i, channels, rows) for i in range(rows)]
    for i in range(rows):
        m_ref[i] = kept[i].astype(BF16)
    even = place_ref[0]
    for k in range(RING):
        first, last = kept[k], kept[rows - RING + k]
        inner_ref[k] = choose(even, last, first).astype(BF16)
        outer_ref[k] = choose(even, first, last).astype(BF16)


def strips_body(
    m_ref, inner_ref, outer_ref, place_ref, south_ref, halo_ref, near_ref, far_ref
):
    rows, channels, cols = m_ref.shape
    here = lax.broadcasted_iota(jnp.int32, (cols, cols), 0)
    there = lax.broadcasted_iota(jnp.int32, (cols, cols), 1)
    flip = (here + there == cols - 1).astype(F32).astype(BF16)
    even, top, lon_even = place_ref[0], place_ref[1], place_ref[2]
    for k in range(RING):
        inner = inner_ref[k].astype(F32)
        outer = outer_ref[k].astype(F32)
        turned = jnp.dot(outer_ref[RING - 1 - k], flip, preferred_element_type=F32)
        south_ref[k] = choose(even, outer, inner).astype(BF16)
        halo_ref[k] = choose(even, inner, choose(top, turned, outer)).astype(BF16)
    lane = lax.broadcasted_iota(jnp.int32, (channels, 128), 1)
    left = jnp.zeros((channels, 128), F32)
    right = jnp.zeros((channels, 128), F32)
    for r in range(rows + 2 * RING):
        if r < RING:
            ref, at = south_ref, r
        elif r < rows + RING:
            ref, at = m_ref, r - RING
        else:
            ref, at = halo_ref, r - RING - rows
        here = (lane >= RING * r) & (lane < RING * r + RING)
        head = ref[at, :, 0:128].astype(F32)
        tail = ref[at, :, cols - 128 : cols].astype(F32)
        if r:
            head = pltpu.roll(head, RING * r, 1)
        tail = pltpu.roll(tail, RING * r + RING, 1)
        left = jnp.where(here, head, left)
        right = jnp.where(here, tail, right)
    near_ref[...] = choose(lon_even, right, left).astype(BF16)
    far_ref[...] = choose(lon_even, left, right).astype(BF16)


def strips_and_sums_body(
    m_ref, inner_ref, outer_ref, sums_ref, place_ref,
    south_ref, halo_ref, near_ref, far_ref, out_ref,
):
    strips_body(
        m_ref, inner_ref, outer_ref, place_ref, south_ref, halo_ref, near_ref, far_ref
    )
    out_ref[...] = sums_ref[...]


def fill(ext, m_ref, south_ref, halo_ref, near_ref, far_ref, lon_even):
    rows, channels, cols = m_ref.shape
    lane = lax.broadcasted_iota(jnp.int32, (channels, 128), 1)
    near = near_ref[...].astype(F32)
    far = far_ref[...].astype(F32)
    before = choose(lon_even, far, near)
    after = choose(lon_even, near, far)
    for r in range(rows + 2 * RING):
        if r < RING:
            row = south_ref[r]
        elif r < rows + RING:
            row = m_ref[r - RING]
        else:
            row = halo_ref[r - RING - rows]
        ext[r, :, 0:cols] = row.astype(F32)
        right = after if r == 0 else pltpu.roll(after, 128 - RING * r, 1)
        left = pltpu.roll(before, 128 - RING - RING * r, 1)
        ext[r, :, cols : cols + 128] = jnp.where(
            lane < RING, right, jnp.where(lane >= 128 - RING, left, 0.0)
        )


def windows(tiles, step, lane):
    if step == 0:
        return tiles[:-1]
    count = len(tiles)
    if step > 0:
        turned = [pltpu.roll(t, 128 - step, 1) for t in tiles]
        keep = lane < 128 - step
        return [jnp.where(keep, turned[t], turned[t + 1]) for t in range(count - 1)]
    turned = [pltpu.roll(t, -step, 1) for t in tiles]
    keep = lane >= -step
    return [jnp.where(keep, turned[t], turned[t - 1]) for t in range(count - 1)]


def tap_columns(dw_ref):
    rows = jnp.concatenate([dw_ref[a] for a in range(7)], axis=0)
    blank = jnp.zeros((128 - rows.shape[0], rows.shape[1]), F32)
    return jnp.concatenate([rows, blank], axis=0).T


def tap(weights, index):
    return jnp.broadcast_to(weights[:, index : index + 1], (8, 128))


def correlate(ext, c0, rows, pairs, lane, weights, top):
    summed = [[None] * pairs for _ in range(rows)]
    for b in range(7):
        if top is None:
            taps = [tap(weights, a * 7 + b) for a in range(7)]
            far = taps
        else:
            taps = [tap(weights, 48 - a * 7 - b) for a in range(7)]
            far = [jnp.where(top, tap(weights, a * 7 + b), taps[a]) for a in range(7)]
        for r in range(rows + 2 * RING):
            tiles = [ext[r, pl.ds(c0, 8), t * 128 : t * 128 + 128] for t in range(pairs + 1)]
            wins = windows(tiles, b - RING, lane)
            for a in range(7):
                i = r - a
                if 0 <= i < rows:
                    weight = far[a] if r >= rows + RING else taps[a]
                    for t in range(pairs):
                        term = weight * wins[t]
                        old = summed[i][t]
                        summed[i][t] = term if old is None else old + term
    return summed


def block_body(
    settle, m_ref, south_ref, halo_ref, near_ref, far_ref, ct_ref, mask_ref,
    dw_ref, gain_ref, w_in_ref, b_ref, w_out_ref, place_ref,
    out_ref, g_ref, inner_ref, outer_ref, wide_ref, tail_ref, ext_ref,
    conv, flat, act, back, sca, pre, b_acc, gain_acc, taps,
):
    ext = ext_ref
    rows, channels, cols = m_ref.shape
    hidden = w_out_ref.shape[0]
    pairs = cols // 128
    fill(ext, m_ref, south_ref, halo_ref, near_ref, far_ref, place_ref[2])
    settle()
    taps[...] = tap_columns(dw_ref)
    sea = mask_ref[...].astype(F32)
    spread(flat, ct_ref[...].astype(F32) * sea[None])
    for i in range(rows):
        back[:, i * cols : i * cols + cols] = row_of(flat, i, channels, rows).astype(BF16)

    def conv_step(ct, carry):
        c0 = pl.multiple_of(ct * 8, 8)
        lane = lanes()
        summed = correlate(ext, c0, rows, pairs, lane, taps[pl.ds(c0, 8), :], None)
        for i in range(rows):
            for t in range(pairs):
                conv[i, pl.ds(c0, 8), t * 128 : t * 128 + 128] = summed[i][t]
        return carry

    lax.fori_loop(0, channels // 8, conv_step, 0)

    b_acc[...] = jnp.zeros_like(b_acc)
    gain_acc[...] = jnp.zeros_like(gain_acc)
    gain = jnp.broadcast_to(gain_ref[...], (128, channels)).T
    gain = jnp.concatenate([gain] * pairs, axis=1)
    bias = jnp.broadcast_to(b_ref[...], (128, hidden)).T
    bias = jnp.concatenate([bias] * pairs, axis=1)
    w_in_t = w_in_ref[...].T
    w_out_t = w_out_ref[...].T
    root = 0.7978845608028654
    for i in range(rows):
        span = slice(i * cols, i * cols + cols)
        raw = conv[i]
        centred = raw - jnp.mean(raw, axis=0, keepdims=True)
        inv_std = lax.rsqrt(jnp.mean(centred * centred, axis=0, keepdims=True) + 1e-06)
        normed = centred * inv_std
        scaled = (normed * gain).astype(BF16)
        sca[:, span] = scaled
        v = jnp.dot(w_in_t, scaled, preferred_element_type=F32) + bias
        v2 = v * v
        t = jnp.tanh(root * v * (1.0 + 0.044715 * v2))
        half = 0.5 * (1.0 + t)
        activated = (v * half).astype(BF16)
        act[:, span] = activated
        slope = half + 0.5 * v * (1.0 - t * t) * (root * (1.0 + 3 * 0.044715 * v2))
        mixed = jnp.dot(w_out_t, activated, preferred_element_type=F32)
        mixed = m_ref[i].astype(F32) + mixed
        for t in range(pairs):
            flat[t, pl.ds(i, channels, stride=rows), :] = mixed[:, t * 128 : t * 128 + 128]
        act_grad = jnp.dot(w_out_ref[...], back[:, span], preferred_element_type=F32)
        pre_grad = (act_grad * slope).astype(BF16)
        pre[:, span] = pre_grad
        wide = pre_grad.astype(F32)
        b_acc[...] += sum(wide[:, t * 128 : t * 128 + 128] for t in range(pairs))
        scaled_grad = jnp.dot(w_in_ref[...], pre_grad, preferred_element_type=F32)
        gains = scaled_grad * normed
        gain_acc[...] += sum(gains[:, t * 128 : t * 128 + 128] for t in range(pairs))
        norm_grad = scaled_grad * gain
        grad = inv_std * (
            norm_grad
            - jnp.mean(norm_grad, axis=0, keepdims=True)
            - normed * jnp.mean(norm_grad * normed, axis=0, keepdims=True)
        )
        g_ref[i] = grad.astype(BF16)

    even = place_ref[0]
    for k in range(RING):
        first, last = g_ref[k].astype(F32), g_ref[rows - RING + k].astype(F32)
        inner_ref[k] = choose(even, last, first).astype(BF16)
        outer_ref[k] = choose(even, first, last).astype(BF16)
    out_ref[...] = (gather(flat, channels, rows) * sea[None]).astype(BF16)
    over_cells = (((1,), (1,)), ((), ()))
    w_in_sum = lax.dot_general(sca[...], pre[...], over_cells, preferred_element_type=F32)
    w_out_sum = lax.dot_general(act[...], back[...], over_cells, preferred_element_type=F32)
    low = channels + hidden
    shift = hidden - 128
    wide_ref[0:channels, :] = w_in_sum[:, 0:128].astype(BF16)
    blank = jnp.zeros((hidden, 128 - channels), F32)
    wide_ref[channels:low, :] = jnp.concatenate([w_out_sum, blank], axis=1).astype(BF16)
    blank = jnp.zeros((channels, 128 - shift), F32)
    tail = jnp.concatenate([w_in_sum[:, 128:hidden], blank], axis=1)
    lane = lax.broadcasted_iota(jnp.int32, (channels, 128), 1)
    tail = jnp.where(lane == shift + 49, jnp.sum(gain_acc[...], axis=1, keepdims=True), tail)
    for part in range(hidden // channels):
        column = jnp.sum(b_acc[part * channels : part * channels + channels, :], axis=1, keepdims=True)
        tail = jnp.where(lane == shift + 50 + part, column, tail)
    tail_ref[...] = tail


def kernel_body(shift, ext, g_ref, wide_ref, tail_ref, sums_ref, tail, grid):
    rows, channels, cols = g_ref.shape
    pairs = cols // 128
    grid[...] = g_ref[...].astype(F32)

    def kernel_step(ct, carry):
        c0 = pl.multiple_of(ct * 8, 8)
        lane = lanes()
        tile = tail_ref[pl.ds(c0, 8), :]
        grads = [
            [grid[i, pl.ds(c0, 8), t * 128 : t * 128 + 128] for t in range(pairs)]
            for i in range(rows)
        ]
        for b in range(7):
            summed = [None] * 7
            for r in range(rows + 2 * RING):
                tiles = [ext[r, pl.ds(c0, 8), t * 128 : t * 128 + 128] for t in range(pairs + 1)]
                wins = windows(tiles, b - RING, lane)
                for a in range(7):
                    i = r - a
                    if 0 <= i < rows:
                        for t in range(pairs):
                            term = grads[i][t] * wins[t]
                            summed[a] = term if summed[a] is None else summed[a] + term
            for a in range(7):
                total = jnp.sum(summed[a], axis=1, keepdims=True)
                tile = jnp.where(lane == shift + a * 7 + b, total, tile)
        tail[pl.ds(c0, 8), :] = tile
        return carry

    lax.fori_loop(0, channels // 8, kernel_step, 0)
    low = wide_ref.shape[0]
    sums_ref[0:low, :] = wide_ref[...]
    sums_ref[low : low + channels, :] = tail[...].astype(BF16)


def back_body(
    settle, g_ref, south_ref, halo_ref, near_ref, far_ref, ct_ref, mask_ref, dw_ref, place_ref,
    out_ref, ext, flat, taps,
):
    rows, channels, cols = g_ref.shape
    pairs = cols // 128
    fill(ext, g_ref, south_ref, halo_ref, near_ref, far_ref, place_ref[2])
    settle()
    taps[...] = tap_columns(dw_ref)

    def step(ct, carry):
        c0 = pl.multiple_of(ct * 8, 8)
        lane = lanes()
        top = jnp.broadcast_to(place_ref[1], (8, 128)) > 0
        summed = correlate(ext, c0, rows, pairs, lane, taps[pl.ds(c0, 8), :], top)
        for i in range(rows):
            for t in range(pairs):
                flat[t, pl.ds(c0 * rows + i, 8, stride=rows), :] = summed[i][t]
        return carry

    lax.fori_loop(0, channels // 8, step, 0)
    sea = mask_ref[...].astype(F32)[None]
    grad = gather(flat, channels, rows) + ct_ref[...].astype(F32) * sea
    out_ref[...] = (grad * sea).astype(BF16)


def lat_halo(inner, outer):
    n_lat, n_lon = lax.axis_size("lat"), lax.axis_size("lon")
    pairs = []
    for i in range(n_lon):
        for j in range(1, n_lat - 1, 2):
            pairs += [(i * n_lat + j, i * n_lat + j + 1), (i * n_lat + j + 1, i * n_lat + j)]
        pairs.append((i * n_lat + n_lat - 1, (n_lon - 1 - i) * n_lat + n_lat - 1))
    outer = lax.ppermute(outer, ("lon", "lat"), pairs)
    inner = lax.ppermute(inner, "lat", [(i, i ^ 1) for i in range(n_lat)])
    return inner, outer


def lon_halo(near, far):
    n_lon = lax.axis_size("lon")
    far = lax.ppermute(far, "lon", [(i, (i - 1 + 2 * (i % 2)) % n_lon) for i in range(n_lon)])
    near = lax.ppermute(near, "lon", [(i, i ^ 1) for i in range(n_lon)])
    return near, far


def held(struct):
    return pltpu.VMEM(struct.shape, struct.dtype)


def like(shape, dtype):
    return jax.ShapeDtypeStruct(shape, dtype)


def spread_body(pieces_ref, out_ref):
    summed = jnp.sum(pieces_ref[...].astype(F32), axis=0).astype(out_ref.dtype)
    for i in range(out_ref.shape[0]):
        out_ref[i] = summed


def unpack_body(scale, sums_ref, w_in_ref, w_out_ref, dw_ref, gain_ref, b_ref):
    channels, hidden = w_in_ref.shape
    low = channels + hidden
    shift = hidden - 128
    tail = sums_ref[low : low + channels, :] * scale
    w_in_ref[...] = jnp.concatenate([sums_ref[0:channels, :] * scale, tail[:, 0:shift]], axis=1)
    w_out_ref[...] = sums_ref[channels:low, 0:channels] * scale
    turned = tail.T
    for a in range(7):
        dw_ref[a] = turned[shift + 7 * a : shift + 7 * a + 7, :]
    gain_ref[...] = turned[shift + 49 : shift + 50, :]
    parts = [turned[shift + 50 + k : shift + 51 + k, :] for k in range(hidden // channels)]
    b_ref[...] = jnp.concatenate(parts, axis=1)


def shards(fields, land_mask, dw_kernel, gain, w_in, b_in, w_out, cotangent):
    channels, rows, cols = fields.shape
    hidden = w_out.shape[0]
    n_lat, n_lon = lax.axis_size("lat"), lax.axis_size("lon")
    taps = dw_kernel.transpose(1, 2, 0)
    lat, lon = lax.axis_index("lat"), lax.axis_index("lon")
    place = jnp.stack([1 - lat % 2, (lat == n_lat - 1).astype(jnp.int32), 1 - lon % 2])
    ring = like((RING, channels, cols), BF16)
    grid = like((rows, channels, cols), BF16)
    whole = like((channels, rows, cols), BF16)
    flat = pltpu.VMEM((cols // 128, channels * rows, 128), F32)
    ext = pltpu.VMEM((rows + 2 * RING, channels, cols + 128), F32)
    near_ring = held(ring)
    strip = pltpu.VMEM((channels, 128), BF16)
    height = 2 * channels + hidden
    near_sums = pltpu.VMEM((height, 128), BF16)
    cells = rows * cols
    masked, inner, outer = call(
        rows_body, [held(grid), near_ring, near_ring], [], [fields, land_mask], [place],
        scratch=[flat],
    )
    inner, outer = lat_halo(inner, outer)
    south, north, near, far = call(
        strips_body, [near_ring, near_ring, strip, strip], [masked, inner, outer], (), [place]
    )
    near, far = lon_halo(near, far)
    columns = pltpu.VMEM((channels, 128), F32)
    output, grads, inner, outer, wide, tail, ext_rows = call(
        block_body,
        [
            whole, held(grid), near_ring, near_ring,
            pltpu.VMEM((height - channels, 128), BF16), columns, ext,
        ],
        [masked, south, north, near, far],
        [
            cotangent, land_mask, taps, gain.reshape(1, channels), w_in,
            b_in.reshape(1, hidden), w_out,
        ],
        [place],
        scratch=[
            pltpu.VMEM((rows, channels, cols), F32),
            flat,
            pltpu.VMEM((hidden, cells), BF16),
            pltpu.VMEM((channels, cells), BF16),
            pltpu.VMEM((channels, cells), BF16),
            pltpu.VMEM((hidden, cells), BF16),
            pltpu.VMEM((hidden, 128), F32),
            columns,
            columns,
        ],
    )
    inner, outer = lat_halo(inner, outer)
    (sums,) = call(
        functools.partial(kernel_body, hidden - 128), [near_sums], [ext_rows, grads, wide, tail],
        scratch=[columns, pltpu.VMEM((rows, channels, cols), F32)],
    )
    south, north, near, far, sums = call(
        strips_and_sums_body, [near_ring, near_ring, strip, strip, near_sums],
        [grads, inner, outer, sums], (), [place],
    )
    near, far = lon_halo(near, far)
    size = height // n_lat
    pieces = lax.all_to_all(sums.reshape(n_lat, size, 128), "lat", 0, 0, tiled=True)
    (pieces,) = call(spread_body, [pltpu.VMEM((n_lon, size, 128), BF16)], [pieces])
    pieces = lax.all_to_all(pieces, "lon", 0, 0, tiled=True)
    (pieces,) = call(
        spread_body, [pltpu.VMEM((n_lat, size, 128), F32)], [pieces], waits=[near, far]
    )
    pieces = lax.all_to_all(pieces, "lat", 0, 0, tiled=True)
    (input_grad,) = call(
        back_body, [whole], [grads, south, north, near, far], [cotangent, land_mask, taps],
        [place], scratch=[ext, flat, columns],
    )
    scale = float(cells * n_lat * n_lon) ** -0.5
    w_in_grad, w_out_grad, dw_grad, gain_grad, b_grad = call(
        functools.partial(unpack_body, scale),
        [
            like((channels, hidden), F32),
            like((hidden, channels), F32),
            like((7, 7, channels), F32),
            like((1, channels), F32),
            like((1, hidden), F32),
        ],
        [pieces.reshape(height, 128)],
    )
    return (
        output,
        input_grad,
        dw_grad.transpose(2, 0, 1),
        gain_grad.reshape(channels),
        w_in_grad,
        b_grad.reshape(hidden),
        w_out_grad,
    )


def solution(mesh):
    tiles = P(None, "lat", "lon")
    return jax.shard_map(
        shards,
        mesh=mesh,
        in_specs=(tiles, P("lat", "lon"), P(), P(), P(), P(), P(), tiles),
        out_specs=(tiles, tiles, P(), P(), P(), P(), P()),
        check_vma=False,
    )
```

```python
import functools

import jax
import jax.numpy as jnp
from jax import lax
from jax.experimental import pallas as pl
from jax.experimental.pallas import tpu as pltpu
from jax.sharding import PartitionSpec as P

F32 = jnp.float32
BF16 = jnp.bfloat16
VMEM_LIMIT = 48 * 1024 * 1024
RING = 3


def call(body, outs, args, raw=(), scalars=(), scratch=(), waits=()):
    count = len(args)
    end = count + len(raw) + len(scalars) + len(waits)
    specs = [pl.BlockSpec(memory_space=pltpu.VMEM)] * count
    specs += [pl.BlockSpec(memory_space=pltpu.HBM)] * len(raw)
    specs += [pl.BlockSpec(memory_space=pltpu.SMEM)] * len(scalars)
    specs += [pl.BlockSpec(memory_space=pl.ANY)] * len(waits)
    near = [pltpu.with_memory_space_constraint(x, pltpu.VMEM) for x in args]
    far = [pltpu.with_memory_space_constraint(x, pltpu.HBM) for x in raw]
    slots = [pltpu.VMEM(x.shape, x.dtype) for x in raw]

    def run(*refs):
        first = end + len(outs)
        made = refs[len(refs) - 1 - len(raw) : len(refs) - 1] if raw else ()
        inner = refs[first : len(refs) - 1 - len(raw)] if raw else refs[first:]
        rest = (*refs[count + len(raw) : end - len(waits)], *refs[end:first], *inner)
        if not raw:
            return body(*refs[:count], *rest)
        copies = [
            pltpu.make_async_copy(refs[count + i], made[i], refs[-1].at[i])
            for i in range(len(raw))
        ]
        for copy in copies:
            copy.start()

        def settle():
            for copy in copies:
                copy.wait()

        return body(settle, *refs[:count], *made, *rest)

    extra = [*slots, pltpu.SemaphoreType.DMA((len(raw),))] if raw else []
    return pl.pallas_call(
        run,
        out_shape=outs,
        in_specs=specs,
        out_specs=[pl.BlockSpec(memory_space=pltpu.VMEM)] * len(outs),
        scratch_shapes=[*scratch, *extra],
        compiler_params=pltpu.CompilerParams(vmem_limit_bytes=VMEM_LIMIT),
    )(*near, *far, *scalars, *waits)


def lanes():
    return lax.broadcasted_iota(jnp.int32, (8, 128), 1)


def spread(flat, values):
    channels, rows, cols = values.shape
    for t in range(cols // 128):
        part = values[:, :, t * 128 : t * 128 + 128]
        flat[t] = part.reshape(channels * rows, 128)


def gather(flat, channels, rows):
    parts = [flat[t].reshape(channels, rows, 128) for t in range(flat.shape[0])]
    return jnp.concatenate(parts, axis=2)


def row_of(flat, i, channels, rows):
    parts = [flat[t, pl.ds(i, channels, stride=rows), :] for t in range(flat.shape[0])]
    return jnp.concatenate(parts, axis=1)


def choose(flag, yes, no):
    return jnp.where(jnp.broadcast_to(flag, yes.shape) > 0, yes, no)


def split_ends(m_ref, even, inner_ref, outer_ref):
    rows = m_ref.shape[0]
    for k in range(RING):
        first, last = m_ref[k].astype(F32), m_ref[rows - RING + k].astype(F32)
        inner_ref[k] = choose(even, last, first).astype(BF16)
        outer_ref[k] = choose(even, first, last).astype(BF16)


def rows_body(settle, f_ref, mask_ref, place_ref, m_ref, inner_ref, outer_ref, flat):
    channels, rows, cols = f_ref.shape
    settle()
    spread(flat, f_ref[...].astype(F32) * mask_ref[...].astype(F32)[None])
    for i in range(rows):
        m_ref[i] = row_of(flat, i, channels, rows).astype(BF16)
    split_ends(m_ref, place_ref[0], inner_ref, outer_ref)


def strips_body(
    m_ref, inner_ref, outer_ref, place_ref, south_ref, halo_ref, near_ref, far_ref
):
    rows, channels, cols = m_ref.shape
    here = lax.broadcasted_iota(jnp.int32, (cols, cols), 0)
    there = lax.broadcasted_iota(jnp.int32, (cols, cols), 1)
    flip = (here + there == cols - 1).astype(F32).astype(BF16)
    even, top, lon_even = place_ref[0], place_ref[1], place_ref[2]
    for k in range(RING):
        inner = inner_ref[k].astype(F32)
        outer = outer_ref[k].astype(F32)
        turned = jnp.dot(outer_ref[RING - 1 - k], flip, preferred_element_type=F32)
        south_ref[k] = choose(even, outer, inner).astype(BF16)
        halo_ref[k] = choose(even, inner, choose(top, turned, outer)).astype(BF16)
    lane = lax.broadcasted_iota(jnp.int32, (channels, 128), 1)
    left = jnp.zeros((channels, 128), F32)
    right = jnp.zeros((channels, 128), F32)
    for r in range(rows + 2 * RING):
        if r < RING:
            ref, at = south_ref, r
        elif r < rows + RING:
            ref, at = m_ref, r - RING
        else:
            ref, at = halo_ref, r - RING - rows
        here = (lane >= RING * r) & (lane < RING * r + RING)
        head = ref[at, :, 0:128].astype(F32)
        tail = ref[at, :, cols - 128 : cols].astype(F32)
        if r:
            head = pltpu.roll(head, RING * r, 1)
        tail = pltpu.roll(tail, RING * r + RING, 1)
        left = jnp.where(here, head, left)
        right = jnp.where(here, tail, right)
    near_ref[...] = choose(lon_even, right, left).astype(BF16)
    far_ref[...] = choose(lon_even, left, right).astype(BF16)


def strips_and_sums_body(
    m_ref, inner_ref, outer_ref, sums_ref, place_ref,
    south_ref, halo_ref, near_ref, far_ref, out_ref,
):
    strips_body(
        m_ref, inner_ref, outer_ref, place_ref, south_ref, halo_ref, near_ref, far_ref
    )
    out_ref[...] = sums_ref[...]


def fill(ext, m_ref, south_ref, halo_ref, near_ref, far_ref, lon_even):
    rows, channels, cols = m_ref.shape
    lane = lax.broadcasted_iota(jnp.int32, (channels, 128), 1)
    near = near_ref[...].astype(F32)
    far = far_ref[...].astype(F32)
    before = choose(lon_even, far, near)
    after = choose(lon_even, near, far)
    for r in range(rows + 2 * RING):
        if r < RING:
            row = south_ref[r]
        elif r < rows + RING:
            row = m_ref[r - RING]
        else:
            row = halo_ref[r - RING - rows]
        ext[r, :, 0:cols] = row.astype(F32)
        right = after if r == 0 else pltpu.roll(after, 128 - RING * r, 1)
        left = pltpu.roll(before, 128 - RING - RING * r, 1)
        ext[r, :, cols : cols + 128] = jnp.where(
            lane < RING, right, jnp.where(lane >= 128 - RING, left, 0.0)
        )


def windows(tiles, step, lane):
    if step == 0:
        return tiles[:-1]
    count = len(tiles)
    shift = 128 - step if step > 0 else -step
    turned = [jnp.zeros((8, 128), F32) if t is None else pltpu.roll(t, shift, 1) for t in tiles]
    if step > 0:
        keep = lane < 128 - step
        return [jnp.where(keep, turned[t], turned[t + 1]) for t in range(count - 1)]
    keep = lane >= -step
    return [jnp.where(keep, turned[t], turned[t - 1]) for t in range(count - 1)]


def tap_columns(dw_ref):
    rows = jnp.concatenate([dw_ref[a] for a in range(7)], axis=0)
    blank = jnp.zeros((128 - rows.shape[0], rows.shape[1]), F32)
    return jnp.concatenate([rows, blank], axis=0).T


def tap(weights, index):
    return jnp.broadcast_to(weights[:, index : index + 1], (8, 128))


def correlate(read, span, rows, lane, weights, flipped, top, summed):
    for b in range(7):
        taps = [tap(weights, 48 - a * 7 - b if flipped else a * 7 + b) for a in range(7)]
        far = taps
        if top is not None:
            far = [jnp.where(top, tap(weights, a * 7 + b), taps[a]) for a in range(7)]
        for r in span:
            wins = windows(read(r), b - RING, lane)
            for a in range(7):
                i = r - a
                if 0 <= i < rows:
                    weight = far[a] if r >= rows + RING else taps[a]
                    for t, win in enumerate(wins):
                        term = weight * win
                        old = summed[i][t]
                        summed[i][t] = term if old is None else old + term
    return summed


def edges(before, after, rows, lane, weights, flipped, top):
    spot = lane % RING
    left = jnp.zeros((8, 128), F32)
    right = jnp.zeros((8, 128), F32)
    for a in range(7):
        for b in (0, 1, 2, 4, 5, 6):
            weight = tap(weights, 48 - a * 7 - b if flipped else a * 7 + b)
            if top is not None and a > RING:
                beyond = top & (lane >= RING * (rows + RING - a))
                weight = jnp.where(beyond, tap(weights, a * 7 + b), weight)
            back = -(RING * a + b) % 128 if b < RING else -(RING * a + b - 6) % 128
            strip = before if b < RING else after
            moved = pltpu.roll(strip, back, 1) if back else strip
            if b < RING:
                left = left + jnp.where(spot <= 2 - b, weight * moved, 0.0)
            else:
                right = right + jnp.where(spot >= 6 - b, weight * moved, 0.0)
    return left, right


def place_edges(left, right, i, lane):
    head = pltpu.roll(left, 128 - RING * i, 1) if i else left
    tail = pltpu.roll(right, 128 - RING - RING * i, 1)
    return jnp.where(lane < RING, head, 0.0), jnp.where(lane >= 128 - RING, tail, 0.0)


def own_body(flipped, settle, m_ref, dw_ref, conv_ref, wide, taps):
    rows, channels, cols = m_ref.shape
    pairs = cols // 128
    wide[...] = m_ref[...].astype(F32)
    settle()
    taps[...] = tap_columns(dw_ref)

    def step(ct, carry):
        c0 = pl.multiple_of(ct * 8, 8)

        def read(r):
            tiles = [wide[r - RING, pl.ds(c0, 8), t * 128 : t * 128 + 128] for t in range(pairs)]
            return tiles + [None]

        blank = [[None] * pairs for _ in range(rows)]
        span = range(RING, rows + RING)
        weights = taps[pl.ds(c0, 8), :]
        summed = correlate(read, span, rows, lanes(), weights, flipped, None, blank)
        for i in range(rows):
            for t in range(pairs):
                conv_ref[i, pl.ds(c0, 8), t * 128 : t * 128 + 128] = summed[i][t]
        return carry

    lax.fori_loop(0, channels // 8, step, 0)


def with_ends(conv_ref, wide, c0, lane, weights, flipped, top):
    rows, channels, cols = conv_ref.shape
    pairs = cols // 128

    def read(r):
        at = r if r < RING else r - rows
        tiles = [wide[at, pl.ds(c0, 8), t * 128 : t * 128 + 128] for t in range(pairs)]
        return tiles + [None]

    summed = [
        [conv_ref[i, pl.ds(c0, 8), t * 128 : t * 128 + 128] for t in range(pairs)]
        for i in range(rows)
    ]
    span = [*range(RING), *range(rows + RING, rows + 2 * RING)]
    return correlate(read, span, rows, lane, weights, flipped, top, summed)


def ends_body(settle, south_ref, halo_ref, conv_ref, dw_ref, out_ref, wide, taps):
    rows, channels, cols = conv_ref.shape
    wide[0:RING] = south_ref[...].astype(F32)
    wide[RING : 2 * RING] = halo_ref[...].astype(F32)
    settle()
    taps[...] = tap_columns(dw_ref)

    def step(ct, carry):
        c0 = pl.multiple_of(ct * 8, 8)
        summed = with_ends(conv_ref, wide, c0, lanes(), taps[pl.ds(c0, 8), :], False, None)
        for i in range(rows):
            for t in range(cols // 128):
                out_ref[i, pl.ds(c0, 8), t * 128 : t * 128 + 128] = summed[i][t]
        return carry

    lax.fori_loop(0, channels // 8, step, 0)


def split_sides(sides, near_ref, far_ref, lon_even):
    near = near_ref[...].astype(F32)
    far = far_ref[...].astype(F32)
    sides[0] = choose(lon_even, far, near)
    sides[1] = choose(lon_even, near, far)


def block_body(
    settle, m_ref, conv_ref, near_ref, far_ref, ct_ref, mask_ref,
    dw_ref, gain_ref, w_in_ref, b_ref, w_out_ref, place_ref,
    out_ref, g_ref, inner_ref, outer_ref, wide_ref, tail_ref,
    conv, flat, act, back, sca, pre, b_acc, gain_acc, taps, sides,
):
    rows, channels, cols = m_ref.shape
    hidden = w_out_ref.shape[0]
    pairs = cols // 128
    split_sides(sides, near_ref, far_ref, place_ref[2])
    settle()
    taps[...] = tap_columns(dw_ref)
    sea = mask_ref[...].astype(F32)
    spread(flat, ct_ref[...].astype(F32) * sea[None])
    for i in range(rows):
        back[:, i * cols : i * cols + cols] = row_of(flat, i, channels, rows).astype(BF16)

    def conv_step(ct, carry):
        c0 = pl.multiple_of(ct * 8, 8)
        lane = lanes()
        before, after = sides[0, pl.ds(c0, 8), :], sides[1, pl.ds(c0, 8), :]
        weights = taps[pl.ds(c0, 8), :]
        left, right = edges(before, after, rows, lane, weights, False, None)
        for i in range(rows):
            head, tail = place_edges(left, right, i, lane)
            for t in range(pairs):
                tile = conv_ref[i, pl.ds(c0, 8), t * 128 : t * 128 + 128]
                if t == 0:
                    tile = tile + head
                if t == pairs - 1:
                    tile = tile + tail
                conv[i, pl.ds(c0, 8), t * 128 : t * 128 + 128] = tile
        return carry

    lax.fori_loop(0, channels // 8, conv_step, 0)

    b_acc[...] = jnp.zeros_like(b_acc)
    gain_acc[...] = jnp.zeros_like(gain_acc)
    gain = jnp.broadcast_to(gain_ref[...], (128, channels)).T
    gain = jnp.concatenate([gain] * pairs, axis=1)
    bias = jnp.broadcast_to(b_ref[...], (128, hidden)).T
    bias = jnp.concatenate([bias] * pairs, axis=1)
    w_in_t = w_in_ref[...].T
    w_out_t = w_out_ref[...].T
    root = 0.7978845608028654
    for i in range(rows):
        span = slice(i * cols, i * cols + cols)
        raw = conv[i]
        centred = raw - jnp.mean(raw, axis=0, keepdims=True)
        inv_std = lax.rsqrt(jnp.mean(centred * centred, axis=0, keepdims=True) + 1e-06)
        normed = centred * inv_std
        scaled = (normed * gain).astype(BF16)
        sca[:, span] = scaled
        v = jnp.dot(w_in_t, scaled, preferred_element_type=F32) + bias
        v2 = v * v
        t = jnp.tanh(root * v * (1.0 + 0.044715 * v2))
        half = 0.5 * (1.0 + t)
        activated = (v * half).astype(BF16)
        act[:, span] = activated
        slope = half + 0.5 * v * (1.0 - t * t) * (root * (1.0 + 3 * 0.044715 * v2))
        mixed = jnp.dot(w_out_t, activated, preferred_element_type=F32)
        mixed = m_ref[i].astype(F32) + mixed
        for t in range(pairs):
            flat[t, pl.ds(i, channels, stride=rows), :] = mixed[:, t * 128 : t * 128 + 128]
        act_grad = jnp.dot(w_out_ref[...], back[:, span], preferred_element_type=F32)
        pre_grad = (act_grad * slope).astype(BF16)
        pre[:, span] = pre_grad
        wide = pre_grad.astype(F32)
        b_acc[...] += sum(wide[:, t * 128 : t * 128 + 128] for t in range(pairs))
        scaled_grad = jnp.dot(w_in_ref[...], pre_grad, preferred_element_type=F32)
        gains = scaled_grad * normed
        gain_acc[...] += sum(gains[:, t * 128 : t * 128 + 128] for t in range(pairs))
        norm_grad = scaled_grad * gain
        grad = inv_std * (
            norm_grad
            - jnp.mean(norm_grad, axis=0, keepdims=True)
            - normed * jnp.mean(norm_grad * normed, axis=0, keepdims=True)
        )
        g_ref[i] = grad.astype(BF16)

    split_ends(g_ref, place_ref[0], inner_ref, outer_ref)
    out_ref[...] = (gather(flat, channels, rows) * sea[None]).astype(BF16)
    over_cells = (((1,), (1,)), ((), ()))
    w_in_sum = lax.dot_general(sca[...], pre[...], over_cells, preferred_element_type=F32)
    w_out_sum = lax.dot_general(act[...], back[...], over_cells, preferred_element_type=F32)
    low = channels + hidden
    shift = hidden - 128
    wide_ref[0:channels, :] = w_in_sum[:, 0:128].astype(BF16)
    blank = jnp.zeros((hidden, 128 - channels), F32)
    wide_ref[channels:low, :] = jnp.concatenate([w_out_sum, blank], axis=1).astype(BF16)
    blank = jnp.zeros((channels, 128 - shift), F32)
    tail = jnp.concatenate([w_in_sum[:, 128:hidden], blank], axis=1)
    lane = lax.broadcasted_iota(jnp.int32, (channels, 128), 1)
    tail = jnp.where(lane == shift + 49, jnp.sum(gain_acc[...], axis=1, keepdims=True), tail)
    for part in range(hidden // channels):
        column = jnp.sum(b_acc[part * channels : part * channels + channels, :], axis=1, keepdims=True)
        tail = jnp.where(lane == shift + 50 + part, column, tail)
    tail_ref[...] = tail


def kernel_body(
    shift, m_ref, south_ref, halo_ref, near_ref, far_ref, g_ref, wide_ref, tail_ref, place_ref,
    sums_ref, tail, grid, ext,
):
    rows, channels, cols = g_ref.shape
    pairs = cols // 128
    fill(ext, m_ref, south_ref, halo_ref, near_ref, far_ref, place_ref[2])
    grid[...] = g_ref[...].astype(F32)

    def kernel_step(ct, carry):
        c0 = pl.multiple_of(ct * 8, 8)
        lane = lanes()
        tile = tail_ref[pl.ds(c0, 8), :]
        grads = [
            [grid[i, pl.ds(c0, 8), t * 128 : t * 128 + 128] for t in range(pairs)]
            for i in range(rows)
        ]
        for b in range(7):
            summed = [None] * 7
            for r in range(rows + 2 * RING):
                tiles = [ext[r, pl.ds(c0, 8), t * 128 : t * 128 + 128] for t in range(pairs + 1)]
                wins = windows(tiles, b - RING, lane)
                for a in range(7):
                    i = r - a
                    if 0 <= i < rows:
                        for t in range(pairs):
                            term = grads[i][t] * wins[t]
                            summed[a] = term if summed[a] is None else summed[a] + term
            for a in range(7):
                total = jnp.sum(summed[a], axis=1, keepdims=True)
                tile = jnp.where(lane == shift + a * 7 + b, total, tile)
        tail[pl.ds(c0, 8), :] = tile
        return carry

    lax.fori_loop(0, channels // 8, kernel_step, 0)
    low = wide_ref.shape[0]
    sums_ref[0:low, :] = wide_ref[...]
    sums_ref[low : low + channels, :] = tail[...].astype(BF16)


def back_body(
    settle, conv_ref, south_ref, halo_ref, near_ref, far_ref, ct_ref, mask_ref, dw_ref, place_ref,
    out_ref, wide, flat, taps, sides,
):
    rows, channels, cols = conv_ref.shape
    pairs = cols // 128
    wide[0:RING] = south_ref[...].astype(F32)
    wide[RING : 2 * RING] = halo_ref[...].astype(F32)
    split_sides(sides, near_ref, far_ref, place_ref[2])
    settle()
    taps[...] = tap_columns(dw_ref)

    def step(ct, carry):
        c0 = pl.multiple_of(ct * 8, 8)
        lane = lanes()
        top = jnp.broadcast_to(place_ref[1], (8, 128)) > 0
        weights = taps[pl.ds(c0, 8), :]
        before, after = sides[0, pl.ds(c0, 8), :], sides[1, pl.ds(c0, 8), :]
        left, right = edges(before, after, rows, lane, weights, True, top)
        summed = with_ends(conv_ref, wide, c0, lane, weights, True, top)
        for i in range(rows):
            head, tail = place_edges(left, right, i, lane)
            for t in range(pairs):
                tile = summed[i][t]
                if t == 0:
                    tile = tile + head
                if t == pairs - 1:
                    tile = tile + tail
                flat[t, pl.ds(c0 * rows + i, 8, stride=rows), :] = tile
        return carry

    lax.fori_loop(0, channels // 8, step, 0)
    sea = mask_ref[...].astype(F32)[None]
    grad = gather(flat, channels, rows) + ct_ref[...].astype(F32) * sea
    out_ref[...] = (grad * sea).astype(BF16)


def lat_halo(inner, outer):
    n_lat, n_lon = lax.axis_size("lat"), lax.axis_size("lon")
    pairs = []
    for i in range(n_lon):
        for j in range(1, n_lat - 1, 2):
            pairs += [(i * n_lat + j, i * n_lat + j + 1), (i * n_lat + j + 1, i * n_lat + j)]
        pairs.append((i * n_lat + n_lat - 1, (n_lon - 1 - i) * n_lat + n_lat - 1))
    outer = lax.ppermute(outer, ("lon", "lat"), pairs)
    inner = lax.ppermute(inner, "lat", [(i, i ^ 1) for i in range(n_lat)])
    return inner, outer


def lon_halo(near, far):
    n_lon = lax.axis_size("lon")
    far = lax.ppermute(far, "lon", [(i, (i - 1 + 2 * (i % 2)) % n_lon) for i in range(n_lon)])
    near = lax.ppermute(near, "lon", [(i, i ^ 1) for i in range(n_lon)])
    return near, far


def held(struct):
    return pltpu.VMEM(struct.shape, struct.dtype)


def like(shape, dtype):
    return jax.ShapeDtypeStruct(shape, dtype)


def spread_body(pieces_ref, out_ref):
    summed = jnp.sum(pieces_ref[...].astype(F32), axis=0).astype(out_ref.dtype)
    for i in range(out_ref.shape[0]):
        out_ref[i] = summed


def unpack_body(scale, sums_ref, w_in_ref, w_out_ref, dw_ref, gain_ref, b_ref):
    channels, hidden = w_in_ref.shape
    low = channels + hidden
    shift = hidden - 128
    tail = sums_ref[low : low + channels, :] * scale
    w_in_ref[...] = jnp.concatenate([sums_ref[0:channels, :] * scale, tail[:, 0:shift]], axis=1)
    w_out_ref[...] = sums_ref[channels:low, 0:channels] * scale
    turned = tail.T
    for a in range(7):
        dw_ref[a] = turned[shift + 7 * a : shift + 7 * a + 7, :]
    gain_ref[...] = turned[shift + 49 : shift + 50, :]
    parts = [turned[shift + 50 + k : shift + 51 + k, :] for k in range(hidden // channels)]
    b_ref[...] = jnp.concatenate(parts, axis=1)


def shards(fields, land_mask, dw_kernel, gain, w_in, b_in, w_out, cotangent):
    channels, rows, cols = fields.shape
    hidden = w_out.shape[0]
    n_lat, n_lon = lax.axis_size("lat"), lax.axis_size("lon")
    taps = dw_kernel.transpose(1, 2, 0)
    lat, lon = lax.axis_index("lat"), lax.axis_index("lon")
    place = jnp.stack([1 - lat % 2, (lat == n_lat - 1).astype(jnp.int32), 1 - lon % 2])
    ring = like((RING, channels, cols), BF16)
    grid = like((rows, channels, cols), BF16)
    whole = like((channels, rows, cols), BF16)
    flat = pltpu.VMEM((cols // 128, channels * rows, 128), F32)
    ext = pltpu.VMEM((rows + 2 * RING, channels, cols + 128), F32)
    near_ring = held(ring)
    strip = pltpu.VMEM((channels, 128), BF16)
    height = 2 * channels + hidden
    near_sums = pltpu.VMEM((height, 128), BF16)
    cells = rows * cols
    masked, inner, outer = call(
        rows_body, [held(grid), near_ring, near_ring], [], [fields, land_mask], [place],
        scratch=[flat],
    )
    inner, outer = lat_halo(inner, outer)
    columns = pltpu.VMEM((channels, 128), F32)
    sides = pltpu.VMEM((2, channels, 128), F32)
    sums_grid = pltpu.VMEM((rows, channels, cols), F32)
    ends = pltpu.VMEM((2 * RING, channels, cols), F32)
    (conv,) = call(
        functools.partial(own_body, False), [sums_grid], [masked], [taps],
        scratch=[sums_grid, columns],
    )
    south, north, near, far = call(
        strips_body, [near_ring, near_ring, strip, strip], [masked, inner, outer], (), [place],
        waits=[conv],
    )
    near, far = lon_halo(near, far)
    (conv,) = call(
        ends_body, [sums_grid], [south, north, conv], [taps], scratch=[ends, columns]
    )
    output, grads, inner, outer, wide, tail = call(
        block_body,
        [
            whole, held(grid), near_ring, near_ring,
            pltpu.VMEM((height - channels, 128), BF16), columns,
        ],
        [masked, conv, near, far],
        [
            cotangent, land_mask, taps, gain.reshape(1, channels), w_in,
            b_in.reshape(1, hidden), w_out,
        ],
        [place],
        scratch=[
            pltpu.VMEM((rows, channels, cols), F32),
            flat,
            pltpu.VMEM((hidden, cells), BF16),
            pltpu.VMEM((channels, cells), BF16),
            pltpu.VMEM((channels, cells), BF16),
            pltpu.VMEM((hidden, cells), BF16),
            pltpu.VMEM((hidden, 128), F32),
            columns,
            columns,
            sides,
        ],
    )
    inner, outer = lat_halo(inner, outer)
    (sums,) = call(
        functools.partial(kernel_body, hidden - 128), [near_sums],
        [masked, south, north, near, far, grads, wide, tail], (), [place],
        scratch=[columns, sums_grid, ext],
    )
    south, north, near, far, sums = call(
        strips_and_sums_body, [near_ring, near_ring, strip, strip, near_sums],
        [grads, inner, outer, sums], (), [place],
    )
    size = height // n_lat
    pieces = lax.all_to_all(sums.reshape(n_lat, size, 128), "lat", 0, 0, tiled=True)
    (conv,) = call(
        functools.partial(own_body, True), [sums_grid], [grads], [taps],
        scratch=[sums_grid, columns], waits=[near],
    )
    (pieces,) = call(
        spread_body, [pltpu.VMEM((n_lon, size, 128), BF16)], [pieces], waits=[conv]
    )
    near, far = lon_halo(near, far)
    pieces = lax.all_to_all(pieces, "lon", 0, 0, tiled=True)
    (pieces,) = call(
        spread_body, [pltpu.VMEM((n_lat, size, 128), F32)], [pieces], waits=[near, far]
    )
    pieces = lax.all_to_all(pieces, "lat", 0, 0, tiled=True)
    (input_grad,) = call(
        back_body, [whole], [conv, south, north, near, far], [cotangent, land_mask, taps],
        [place], scratch=[ends, flat, columns, sides],
    )
    scale = float(cells * n_lat * n_lon) ** -0.5
    w_in_grad, w_out_grad, dw_grad, gain_grad, b_grad = call(
        functools.partial(unpack_body, scale),
        [
            like((channels, hidden), F32),
            like((hidden, channels), F32),
            like((7, 7, channels), F32),
            like((1, channels), F32),
            like((1, hidden), F32),
        ],
        [pieces.reshape(height, 128)],
    )
    return (
        output,
        input_grad,
        dw_grad.transpose(2, 0, 1),
        gain_grad.reshape(channels),
        w_in_grad,
        b_grad.reshape(hidden),
        w_out_grad,
    )


def solution(mesh):
    tiles = P(None, "lat", "lon")
    return jax.shard_map(
        shards,
        mesh=mesh,
        in_specs=(tiles, P("lat", "lon"), P(), P(), P(), P(), P(), tiles),
        out_specs=(tiles, tiles, P(), P(), P(), P(), P()),
        check_vma=False,
    )
```

```python
import functools

import jax
import jax.numpy as jnp
from jax import lax
from jax.experimental import pallas as pl
from jax.experimental.pallas import tpu as pltpu
from jax.sharding import PartitionSpec as P

F32 = jnp.float32
BF16 = jnp.bfloat16
VMEM_LIMIT = 24 * 1024 * 1024
RING = 3


def call(body, outs, args, raw=(), scalars=(), scratch=(), waits=()):
    count = len(args)
    end = count + len(raw) + len(scalars) + len(waits)
    specs = [pl.BlockSpec(memory_space=pltpu.VMEM)] * count
    specs += [pl.BlockSpec(memory_space=pltpu.HBM)] * len(raw)
    specs += [pl.BlockSpec(memory_space=pltpu.SMEM)] * len(scalars)
    specs += [pl.BlockSpec(memory_space=pl.ANY)] * len(waits)
    near = [pltpu.with_memory_space_constraint(x, pltpu.VMEM) for x in args]
    far = [pltpu.with_memory_space_constraint(x, pltpu.HBM) for x in raw]
    slots = [pltpu.VMEM(x.shape, x.dtype) for x in raw]

    def run(*refs):
        first = end + len(outs)
        made = refs[len(refs) - 1 - len(raw) : len(refs) - 1] if raw else ()
        inner = refs[first : len(refs) - 1 - len(raw)] if raw else refs[first:]
        rest = (*refs[count + len(raw) : end - len(waits)], *refs[end:first], *inner)
        if not raw:
            return body(*refs[:count], *rest)
        copies = [
            pltpu.make_async_copy(refs[count + i], made[i], refs[-1].at[i])
            for i in range(len(raw))
        ]
        for copy in copies:
            copy.start()

        def settle():
            for copy in copies:
                copy.wait()

        return body(settle, *refs[:count], *made, *rest)

    extra = [*slots, pltpu.SemaphoreType.DMA((len(raw),))] if raw else []
    return pl.pallas_call(
        run,
        out_shape=outs,
        in_specs=specs,
        out_specs=[pl.BlockSpec(memory_space=pltpu.VMEM)] * len(outs),
        scratch_shapes=[*scratch, *extra],
        compiler_params=pltpu.CompilerParams(vmem_limit_bytes=VMEM_LIMIT),
    )(*near, *far, *scalars, *waits)


def lanes():
    return lax.broadcasted_iota(jnp.int32, (8, 128), 1)


def spread(flat, values):
    channels, rows, cols = values.shape
    for t in range(cols // 128):
        part = values[:, :, t * 128 : t * 128 + 128]
        flat[t] = part.reshape(channels * rows, 128)


def gather(flat, channels, rows):
    parts = [flat[t].reshape(channels, rows, 128) for t in range(flat.shape[0])]
    return jnp.concatenate(parts, axis=2)


def row_of(flat, i, channels, rows):
    parts = [flat[t, pl.ds(i, channels, stride=rows), :] for t in range(flat.shape[0])]
    return jnp.concatenate(parts, axis=1)


def choose(flag, yes, no):
    return jnp.where(jnp.broadcast_to(flag, yes.shape) > 0, yes, no)


def split_ends(m_ref, even, inner_ref, outer_ref):
    rows = m_ref.shape[0]
    for k in range(RING):
        first, last = m_ref[k].astype(F32), m_ref[rows - RING + k].astype(F32)
        inner_ref[k] = choose(even, last, first).astype(BF16)
        outer_ref[k] = choose(even, first, last).astype(BF16)


def rows_body(settle, f_ref, mask_ref, place_ref, m_ref, inner_ref, outer_ref, flat):
    channels, rows, cols = f_ref.shape
    settle()
    spread(flat, f_ref[...].astype(F32) * mask_ref[...].astype(F32)[None])
    for i in range(rows):
        m_ref[i] = row_of(flat, i, channels, rows).astype(BF16)
    split_ends(m_ref, place_ref[0], inner_ref, outer_ref)


def strips_body(
    m_ref, outer_ref, inner_ref, place_ref, south_ref, halo_ref, near_ref, far_ref
):
    rows, channels, cols = m_ref.shape
    here = lax.broadcasted_iota(jnp.int32, (cols, cols), 0)
    there = lax.broadcasted_iota(jnp.int32, (cols, cols), 1)
    flip = (here + there == cols - 1).astype(F32).astype(BF16)
    even, top, lon_even = place_ref[0], place_ref[1], place_ref[2]
    for k in range(RING):
        inner = inner_ref[k].astype(F32)
        outer = outer_ref[k].astype(F32)
        turned = jnp.dot(outer_ref[RING - 1 - k], flip, preferred_element_type=F32)
        south_ref[k] = choose(even, outer, inner).astype(BF16)
        halo_ref[k] = choose(even, inner, choose(top, turned, outer)).astype(BF16)
    lane = lax.broadcasted_iota(jnp.int32, (channels, 128), 1)
    left = jnp.zeros((channels, 128), F32)
    right = jnp.zeros((channels, 128), F32)
    for r in range(rows + 2 * RING):
        if r < RING:
            ref, at = south_ref, r
        elif r < rows + RING:
            ref, at = m_ref, r - RING
        else:
            ref, at = halo_ref, r - RING - rows
        here = (lane >= RING * r) & (lane < RING * r + RING)
        head = ref[at, :, 0:128].astype(F32)
        tail = ref[at, :, cols - 128 : cols].astype(F32)
        if r:
            head = pltpu.roll(head, RING * r, 1)
        tail = pltpu.roll(tail, RING * r + RING, 1)
        left = jnp.where(here, head, left)
        right = jnp.where(here, tail, right)
    near_ref[...] = choose(lon_even, right, left).astype(BF16)
    far_ref[...] = choose(lon_even, left, right).astype(BF16)


def strips_and_sums_body(
    m_ref, outer_ref, inner_ref, sums_ref, place_ref,
    south_ref, halo_ref, near_ref, far_ref, out_ref,
):
    strips_body(
        m_ref, outer_ref, inner_ref, place_ref, south_ref, halo_ref, near_ref, far_ref
    )
    out_ref[...] = sums_ref[...]


def fill(ext, m_ref, south_ref, halo_ref, near_ref, far_ref, lon_even):
    rows, channels, cols = m_ref.shape
    lane = lax.broadcasted_iota(jnp.int32, (channels, 128), 1)
    near = near_ref[...].astype(F32)
    far = far_ref[...].astype(F32)
    before = choose(lon_even, far, near)
    after = choose(lon_even, near, far)
    for r in range(rows + 2 * RING):
        if r < RING:
            row = south_ref[r]
        elif r < rows + RING:
            row = m_ref[r - RING]
        else:
            row = halo_ref[r - RING - rows]
        ext[r, :, 0:cols] = row.astype(F32)
        right = after if r == 0 else pltpu.roll(after, 128 - RING * r, 1)
        left = pltpu.roll(before, 128 - RING - RING * r, 1)
        ext[r, :, cols : cols + 128] = jnp.where(
            lane < RING, right, jnp.where(lane >= 128 - RING, left, 0.0)
        )


def windows(tiles, step, lane):
    if step == 0:
        return tiles[:-1]
    count = len(tiles)
    shift = 128 - step if step > 0 else -step
    turned = [jnp.zeros((8, 128), F32) if t is None else pltpu.roll(t, shift, 1) for t in tiles]
    if step > 0:
        keep = lane < 128 - step
        return [jnp.where(keep, turned[t], turned[t + 1]) for t in range(count - 1)]
    keep = lane >= -step
    return [jnp.where(keep, turned[t], turned[t - 1]) for t in range(count - 1)]


def tap_columns(dw_ref):
    rows = jnp.concatenate([dw_ref[a] for a in range(7)], axis=0)
    blank = jnp.zeros((128 - rows.shape[0], rows.shape[1]), F32)
    return jnp.concatenate([rows, blank], axis=0).T


def tap_tiles(taps, c0):
    return lambda index: taps[index, pl.ds(c0, 8), :]


def correlate(read, span, rows, lane, weights, flipped, top, summed):
    for b in range(7):
        taps = [weights(48 - a * 7 - b if flipped else a * 7 + b) for a in range(7)]
        far = taps
        if top is not None:
            far = [jnp.where(top, weights(a * 7 + b), taps[a]) for a in range(7)]
        for r in span:
            wins = windows(read(r), b - RING, lane)
            for a in range(7):
                i = r - a
                if 0 <= i < rows:
                    weight = far[a] if r >= rows + RING else taps[a]
                    for t, win in enumerate(wins):
                        term = weight * win
                        old = summed[i][t]
                        summed[i][t] = term if old is None else old + term
    return summed


def edges(before, after, rows, lane, weights, flipped, top):
    spot = lane % RING
    left = jnp.zeros((8, 128), F32)
    right = jnp.zeros((8, 128), F32)
    for a in range(7):
        for b in (0, 1, 2, 4, 5, 6):
            weight = weights(48 - a * 7 - b if flipped else a * 7 + b)
            if top is not None and a > RING:
                beyond = top & (lane >= RING * (rows + RING - a))
                weight = jnp.where(beyond, weights(a * 7 + b), weight)
            back = -(RING * a + b) % 128 if b < RING else -(RING * a + b - 6) % 128
            strip = before if b < RING else after
            moved = pltpu.roll(strip, back, 1) if back else strip
            if b < RING:
                left = left + jnp.where(spot <= 2 - b, weight * moved, 0.0)
            else:
                right = right + jnp.where(spot >= 6 - b, weight * moved, 0.0)
    return left, right


def place_edges(left, right, i, lane):
    head = pltpu.roll(left, 128 - RING * i, 1) if i else left
    tail = pltpu.roll(right, 128 - RING - RING * i, 1)
    return jnp.where(lane < RING, head, 0.0), jnp.where(lane >= 128 - RING, tail, 0.0)


def spread_taps(dw_ref, taps_ref):
    columns = tap_columns(dw_ref)
    for k in range(49):
        taps_ref[k] = jnp.broadcast_to(columns[:, k : k + 1], columns.shape)


def first_body(flipped, settle, m_ref, dw_ref, conv_ref, taps_ref, wide):
    settle()
    spread_taps(dw_ref, taps_ref)
    own_body(flipped, m_ref, taps_ref, conv_ref, wide)


def own_body(flipped, m_ref, taps, conv_ref, wide):
    rows, channels, cols = m_ref.shape
    pairs = cols // 128
    wide[...] = m_ref[...].astype(F32)

    def step(ct, carry):
        c0 = pl.multiple_of(ct * 8, 8)

        def read(r):
            tiles = [wide[r - RING, pl.ds(c0, 8), t * 128 : t * 128 + 128] for t in range(pairs)]
            return tiles + [None]

        blank = [[None] * pairs for _ in range(rows)]
        span = range(RING, rows + RING)
        weights = tap_tiles(taps, c0)
        summed = correlate(read, span, rows, lanes(), weights, flipped, None, blank)
        for i in range(rows):
            for t in range(pairs):
                conv_ref[i, pl.ds(c0, 8), t * 128 : t * 128 + 128] = summed[i][t]
        return carry

    lax.fori_loop(0, channels // 8, step, 0)


def with_ends(conv_ref, wide, c0, lane, weights, flipped, top):
    rows, channels, cols = conv_ref.shape
    pairs = cols // 128

    def read(r):
        at = r if r < RING else r - rows
        tiles = [wide[at, pl.ds(c0, 8), t * 128 : t * 128 + 128] for t in range(pairs)]
        return tiles + [None]

    summed = [
        [conv_ref[i, pl.ds(c0, 8), t * 128 : t * 128 + 128] for t in range(pairs)]
        for i in range(rows)
    ]
    span = [*range(RING), *range(rows + RING, rows + 2 * RING)]
    return correlate(read, span, rows, lane, weights, flipped, top, summed)


def ends_body(south_ref, halo_ref, conv_ref, taps, out_ref, wide):
    rows, channels, cols = conv_ref.shape
    wide[0:RING] = south_ref[...].astype(F32)
    wide[RING : 2 * RING] = halo_ref[...].astype(F32)

    def step(ct, carry):
        c0 = pl.multiple_of(ct * 8, 8)
        weights = tap_tiles(taps, c0)
        summed = with_ends(conv_ref, wide, c0, lanes(), weights, False, None)
        for i in range(rows):
            for t in range(cols // 128):
                out_ref[i, pl.ds(c0, 8), t * 128 : t * 128 + 128] = summed[i][t]
        return carry

    lax.fori_loop(0, channels // 8, step, 0)


def split_sides(sides, near_ref, far_ref, lon_even):
    near = near_ref[...].astype(F32)
    far = far_ref[...].astype(F32)
    sides[0] = choose(lon_even, far, near)
    sides[1] = choose(lon_even, near, far)


def block_body(
    settle, m_ref, conv_ref, far_ref, near_ref, taps, ct_ref, mask_ref,
    gain_ref, w_in_ref, b_ref, w_out_ref, place_ref,
    out_ref, g_ref, inner_ref, outer_ref, wide_ref, tail_ref,
    conv, flat, act, back, sca, pre, b_acc, gain_acc, sides,
):
    rows, channels, cols = m_ref.shape
    hidden = w_out_ref.shape[0]
    pairs = cols // 128
    split_sides(sides, near_ref, far_ref, place_ref[2])
    settle()
    sea = mask_ref[...].astype(F32)
    spread(flat, ct_ref[...].astype(F32) * sea[None])
    for i in range(rows):
        back[:, i * cols : i * cols + cols] = row_of(flat, i, channels, rows).astype(BF16)

    def conv_step(ct, carry):
        c0 = pl.multiple_of(ct * 8, 8)
        lane = lanes()
        before, after = sides[0, pl.ds(c0, 8), :], sides[1, pl.ds(c0, 8), :]
        weights = tap_tiles(taps, c0)
        left, right = edges(before, after, rows, lane, weights, False, None)
        for i in range(rows):
            head, tail = place_edges(left, right, i, lane)
            for t in range(pairs):
                tile = conv_ref[i, pl.ds(c0, 8), t * 128 : t * 128 + 128]
                if t == 0:
                    tile = tile + head
                if t == pairs - 1:
                    tile = tile + tail
                conv[i, pl.ds(c0, 8), t * 128 : t * 128 + 128] = tile
        return carry

    lax.fori_loop(0, channels // 8, conv_step, 0)

    b_acc[...] = jnp.zeros_like(b_acc)
    gain_acc[...] = jnp.zeros_like(gain_acc)
    gain = jnp.broadcast_to(gain_ref[...], (128, channels)).T
    gain = jnp.concatenate([gain] * pairs, axis=1)
    bias = jnp.broadcast_to(b_ref[...], (128, hidden)).T
    bias = jnp.concatenate([bias] * pairs, axis=1)
    w_in_t = w_in_ref[...].T
    w_out_t = w_out_ref[...].T
    root = 0.7978845608028654
    for i in range(rows):
        span = slice(i * cols, i * cols + cols)
        raw = conv[i]
        centred = raw - jnp.mean(raw, axis=0, keepdims=True)
        inv_std = lax.rsqrt(jnp.mean(centred * centred, axis=0, keepdims=True) + 1e-06)
        normed = centred * inv_std
        scaled = (normed * gain).astype(BF16)
        sca[:, span] = scaled
        v = jnp.dot(w_in_t, scaled, preferred_element_type=F32) + bias
        v2 = v * v
        t = jnp.tanh(root * v * (1.0 + 0.044715 * v2))
        half = 0.5 * (1.0 + t)
        activated = (v * half).astype(BF16)
        act[:, span] = activated
        slope = half + 0.5 * v * (1.0 - t * t) * (root * (1.0 + 3 * 0.044715 * v2))
        mixed = jnp.dot(w_out_t, activated, preferred_element_type=F32)
        mixed = m_ref[i].astype(F32) + mixed
        for t in range(pairs):
            flat[t, pl.ds(i, channels, stride=rows), :] = mixed[:, t * 128 : t * 128 + 128]
        act_grad = jnp.dot(w_out_ref[...], back[:, span], preferred_element_type=F32)
        pre_grad = (act_grad * slope).astype(BF16)
        pre[:, span] = pre_grad
        wide = pre_grad.astype(F32)
        b_acc[...] += sum(wide[:, t * 128 : t * 128 + 128] for t in range(pairs))
        scaled_grad = jnp.dot(w_in_ref[...], pre_grad, preferred_element_type=F32)
        gains = scaled_grad * normed
        gain_acc[...] += sum(gains[:, t * 128 : t * 128 + 128] for t in range(pairs))
        norm_grad = scaled_grad * gain
        grad = inv_std * (
            norm_grad
            - jnp.mean(norm_grad, axis=0, keepdims=True)
            - normed * jnp.mean(norm_grad * normed, axis=0, keepdims=True)
        )
        g_ref[i] = grad.astype(BF16)

    split_ends(g_ref, place_ref[0], inner_ref, outer_ref)
    out_ref[...] = (gather(flat, channels, rows) * sea[None]).astype(BF16)
    over_cells = (((1,), (1,)), ((), ()))
    w_in_sum = lax.dot_general(sca[...], pre[...], over_cells, preferred_element_type=F32)
    w_out_sum = lax.dot_general(act[...], back[...], over_cells, preferred_element_type=F32)
    low = channels + hidden
    shift = hidden - 128
    wide_ref[0:channels, :] = w_in_sum[:, 0:128].astype(BF16)
    blank = jnp.zeros((hidden, 128 - channels), F32)
    wide_ref[channels:low, :] = jnp.concatenate([w_out_sum, blank], axis=1).astype(BF16)
    blank = jnp.zeros((channels, 128 - shift), F32)
    tail = jnp.concatenate([w_in_sum[:, 128:hidden], blank], axis=1)
    lane = lax.broadcasted_iota(jnp.int32, (channels, 128), 1)
    tail = jnp.where(lane == shift + 49, jnp.sum(gain_acc[...], axis=1, keepdims=True), tail)
    for part in range(hidden // channels):
        column = jnp.sum(b_acc[part * channels : part * channels + channels, :], axis=1, keepdims=True)
        tail = jnp.where(lane == shift + 50 + part, column, tail)
    tail_ref[...] = tail


def kernel_body(
    shift, m_ref, south_ref, halo_ref, near_ref, far_ref, g_ref, wide_ref, tail_ref, place_ref,
    sums_ref, tail, grid, ext, held_sums,
):
    rows, channels, cols = g_ref.shape
    pairs = cols // 128
    fill(ext, m_ref, south_ref, halo_ref, near_ref, far_ref, place_ref[2])
    grid[...] = g_ref[...].astype(F32)

    def kernel_step(ct, carry):
        c0 = pl.multiple_of(ct * 8, 8)
        lane = lanes()
        grads = [
            [grid[i, pl.ds(c0, 8), t * 128 : t * 128 + 128] for t in range(pairs)]
            for i in range(rows)
        ]
        for b in range(7):
            summed = [None] * 7
            for r in range(rows + 2 * RING):
                tiles = [ext[r, pl.ds(c0, 8), t * 128 : t * 128 + 128] for t in range(pairs + 1)]
                wins = windows(tiles, b - RING, lane)
                for a in range(7):
                    i = r - a
                    if 0 <= i < rows:
                        for t in range(pairs):
                            term = grads[i][t] * wins[t]
                            summed[a] = term if summed[a] is None else summed[a] + term
            for a in range(7):
                held_sums[a * 7 + b, pl.ds(c0, 8), :] = summed[a]
        return carry

    lax.fori_loop(0, channels // 8, kernel_step, 0)
    tail[...] = tail_ref[...]
    lane = lax.broadcasted_iota(jnp.int32, (channels, 128), 1)
    ones = jnp.ones((256, 128), BF16)
    for k in range(49):
        high = held_sums[k].astype(BF16)
        low_part = (held_sums[k] - high.astype(F32)).astype(BF16)
        both = jnp.concatenate([high, low_part], axis=1)
        over_lanes = jnp.dot(both, ones, preferred_element_type=F32)
        tail[...] = jnp.where(lane == shift + k, over_lanes, tail[...])
    low = wide_ref.shape[0]
    sums_ref[0:low, :] = wide_ref[...]
    sums_ref[low : low + channels, :] = tail[...].astype(BF16)


def back_body(
    settle, conv_ref, south_ref, halo_ref, near_ref, far_ref, ct_ref, mask_ref, dw_ref, place_ref,
    out_ref, wide, flat, sides, taps,
):
    rows, channels, cols = conv_ref.shape
    pairs = cols // 128
    wide[0:RING] = south_ref[...].astype(F32)
    wide[RING : 2 * RING] = halo_ref[...].astype(F32)
    split_sides(sides, near_ref, far_ref, place_ref[2])
    settle()
    spread_taps(dw_ref, taps)

    def step(ct, carry):
        c0 = pl.multiple_of(ct * 8, 8)
        lane = lanes()
        top = jnp.broadcast_to(place_ref[1], (8, 128)) > 0
        weights = tap_tiles(taps, c0)
        before, after = sides[0, pl.ds(c0, 8), :], sides[1, pl.ds(c0, 8), :]
        left, right = edges(before, after, rows, lane, weights, True, top)
        summed = with_ends(conv_ref, wide, c0, lane, weights, True, top)
        for i in range(rows):
            head, tail = place_edges(left, right, i, lane)
            for t in range(pairs):
                tile = summed[i][t]
                if t == 0:
                    tile = tile + head
                if t == pairs - 1:
                    tile = tile + tail
                flat[t, pl.ds(c0 * rows + i, 8, stride=rows), :] = tile
        return carry

    lax.fori_loop(0, channels // 8, step, 0)
    sea = mask_ref[...].astype(F32)[None]
    grad = gather(flat, channels, rows) + ct_ref[...].astype(F32) * sea
    out_ref[...] = (grad * sea).astype(BF16)


def lat_halo(inner, outer):
    n_lat, n_lon = lax.axis_size("lat"), lax.axis_size("lon")
    pairs = []
    for i in range(n_lon):
        for j in range(1, n_lat - 1, 2):
            pairs += [(i * n_lat + j, i * n_lat + j + 1), (i * n_lat + j + 1, i * n_lat + j)]
        pairs.append((i * n_lat + n_lat - 1, (n_lon - 1 - i) * n_lat + n_lat - 1))
    outer = lax.ppermute(outer, ("lon", "lat"), pairs)
    inner = lax.ppermute(inner, "lat", [(i, i ^ 1) for i in range(n_lat)])
    return inner, outer


def lon_halo(near, far):
    n_lon = lax.axis_size("lon")
    far = lax.ppermute(far, "lon", [(i, (i - 1 + 2 * (i % 2)) % n_lon) for i in range(n_lon)])
    near = lax.ppermute(near, "lon", [(i, i ^ 1) for i in range(n_lon)])
    return near, far


def held(struct):
    return pltpu.VMEM(struct.shape, struct.dtype)


def like(shape, dtype):
    return jax.ShapeDtypeStruct(shape, dtype)


def spread_body(pieces_ref, out_ref):
    summed = jnp.sum(pieces_ref[...].astype(F32), axis=0).astype(out_ref.dtype)
    for i in range(out_ref.shape[0]):
        out_ref[i] = summed


def unpack_body(scale, sums_ref, w_in_ref, w_out_ref, dw_ref, gain_ref, b_ref):
    channels, hidden = w_in_ref.shape
    low = channels + hidden
    shift = hidden - 128
    tail = sums_ref[low : low + channels, :] * scale
    w_in_ref[...] = jnp.concatenate([sums_ref[0:channels, :] * scale, tail[:, 0:shift]], axis=1)
    w_out_ref[...] = sums_ref[channels:low, 0:channels] * scale
    turned = tail.T
    for a in range(7):
        dw_ref[a] = turned[shift + 7 * a : shift + 7 * a + 7, :]
    gain_ref[...] = turned[shift + 49 : shift + 50, :]
    parts = [turned[shift + 50 + k : shift + 51 + k, :] for k in range(hidden // channels)]
    b_ref[...] = jnp.concatenate(parts, axis=1)


def shards(fields, land_mask, dw_kernel, gain, w_in, b_in, w_out, cotangent):
    channels, rows, cols = fields.shape
    hidden = w_out.shape[0]
    n_lat, n_lon = lax.axis_size("lat"), lax.axis_size("lon")
    taps = dw_kernel.transpose(1, 2, 0)
    lat, lon = lax.axis_index("lat"), lax.axis_index("lon")
    place = jnp.stack([1 - lat % 2, (lat == n_lat - 1).astype(jnp.int32), 1 - lon % 2])
    ring = like((RING, channels, cols), BF16)
    grid = like((rows, channels, cols), BF16)
    whole = like((channels, rows, cols), BF16)
    flat = pltpu.VMEM((cols // 128, channels * rows, 128), F32)
    ext = pltpu.VMEM((rows + 2 * RING, channels, cols + 128), F32)
    near_ring = held(ring)
    strip = pltpu.VMEM((channels, 128), BF16)
    height = 2 * channels + hidden
    near_sums = pltpu.VMEM((height, 128), BF16)
    cells = rows * cols
    masked, inner, outer = call(
        rows_body, [held(grid), near_ring, near_ring], [], [fields, land_mask], [place],
        scratch=[flat],
    )
    inner, outer = lat_halo(inner, outer)
    columns = pltpu.VMEM((channels, 128), F32)
    sides = pltpu.VMEM((2, channels, 128), F32)
    sums_grid = pltpu.VMEM((rows, channels, cols), F32)
    ends = pltpu.VMEM((2 * RING, channels, cols), F32)
    tap_grid = pltpu.VMEM((49, channels, 128), F32)
    conv, tiles = call(
        functools.partial(first_body, False), [sums_grid, tap_grid], [masked], [taps],
        scratch=[sums_grid],
    )
    south, north, near, far = call(
        strips_body, [near_ring, near_ring, strip, strip], [masked, outer, inner], (), [place],
        waits=[conv],
    )
    near, far = lon_halo(near, far)
    (conv,) = call(
        ends_body, [sums_grid], [south, north, conv, tiles], scratch=[ends]
    )
    output, grads, inner, outer, wide, tail = call(
        block_body,
        [
            whole, held(grid), near_ring, near_ring,
            pltpu.VMEM((height - channels, 128), BF16), columns,
        ],
        [masked, conv, far, near, tiles],
        [
            cotangent, land_mask, gain.reshape(1, channels), w_in,
            b_in.reshape(1, hidden), w_out,
        ],
        [place],
        scratch=[
            pltpu.VMEM((rows, channels, cols), F32),
            flat,
            pltpu.VMEM((hidden, cells), BF16),
            pltpu.VMEM((channels, cells), BF16),
            pltpu.VMEM((channels, cells), BF16),
            pltpu.VMEM((hidden, cells), BF16),
            pltpu.VMEM((hidden, 128), F32),
            columns,
            sides,
        ],
    )
    inner, outer = lat_halo(inner, outer)
    (sums,) = call(
        functools.partial(kernel_body, hidden - 128), [near_sums],
        [masked, south, north, near, far, grads, wide, tail], (), [place],
        scratch=[columns, sums_grid, ext, tap_grid],
    )
    south, north, near, far, sums = call(
        strips_and_sums_body, [near_ring, near_ring, strip, strip, near_sums],
        [grads, outer, inner, sums], (), [place],
    )
    size = height // n_lat
    pieces = lax.all_to_all(sums.reshape(n_lat, size, 128), "lat", 0, 0, tiled=True)
    (conv,) = call(
        functools.partial(first_body, True), [sums_grid], [grads], [taps],
        scratch=[tap_grid, sums_grid], waits=[near],
    )
    (pieces,) = call(
        spread_body, [pltpu.VMEM((n_lon, size, 128), BF16)], [pieces], waits=[conv]
    )
    near, far = lon_halo(near, far)
    pieces = lax.all_to_all(pieces, "lon", 0, 0, tiled=True)
    (pieces,) = call(
        spread_body, [pltpu.VMEM((n_lat, size, 128), F32)], [pieces], waits=[near, far]
    )
    pieces = lax.all_to_all(pieces, "lat", 0, 0, tiled=True)
    (input_grad,) = call(
        back_body, [whole], [conv, south, north, near, far], [cotangent, land_mask, taps],
        [place], scratch=[ends, flat, sides, tap_grid],
    )
    scale = float(cells * n_lat * n_lon) ** -0.5
    w_in_grad, w_out_grad, dw_grad, gain_grad, b_grad = call(
        functools.partial(unpack_body, scale),
        [
            like((channels, hidden), F32),
            like((hidden, channels), F32),
            like((7, 7, channels), F32),
            like((1, channels), F32),
            like((1, hidden), F32),
        ],
        [pieces.reshape(height, 128)],
    )
    return (
        output,
        input_grad,
        dw_grad.transpose(2, 0, 1),
        gain_grad.reshape(channels),
        w_in_grad,
        b_grad.reshape(hidden),
        w_out_grad,
    )


def solution(mesh):
    tiles = P(None, "lat", "lon")
    return jax.shard_map(
        shards,
        mesh=mesh,
        in_specs=(tiles, P("lat", "lon"), P(), P(), P(), P(), P(), tiles),
        out_specs=(tiles, tiles, P(), P(), P(), P(), P()),
        check_vma=False,
    )
```

```python
import functools

import jax
import jax.numpy as jnp
from jax import lax
from jax.experimental import pallas as pl
from jax.experimental.pallas import tpu as pltpu
from jax.sharding import PartitionSpec as P

F32 = jnp.float32
BF16 = jnp.bfloat16
VMEM_LIMIT = 24 * 1024 * 1024
RING = 3


def call(body, outs, args, raw=(), scalars=(), scratch=(), waits=()):
    count = len(args)
    end = count + len(raw) + len(scalars) + len(waits)
    specs = [pl.BlockSpec(memory_space=pltpu.VMEM)] * count
    specs += [pl.BlockSpec(memory_space=pltpu.HBM)] * len(raw)
    specs += [pl.BlockSpec(memory_space=pltpu.SMEM)] * len(scalars)
    specs += [pl.BlockSpec(memory_space=pl.ANY)] * len(waits)
    near = [pltpu.with_memory_space_constraint(x, pltpu.VMEM) for x in args]
    far = [pltpu.with_memory_space_constraint(x, pltpu.HBM) for x in raw]
    slots = [pltpu.VMEM(x.shape, x.dtype) for x in raw]

    def run(*refs):
        first = end + len(outs)
        made = refs[len(refs) - 1 - len(raw) : len(refs) - 1] if raw else ()
        inner = refs[first : len(refs) - 1 - len(raw)] if raw else refs[first:]
        rest = (*refs[count + len(raw) : end - len(waits)], *refs[end:first], *inner)
        if not raw:
            return body(*refs[:count], *rest)
        copies = [
            pltpu.make_async_copy(refs[count + i], made[i], refs[-1].at[i])
            for i in range(len(raw))
        ]
        for copy in copies:
            copy.start()

        def settle():
            for copy in copies:
                copy.wait()

        return body(settle, *refs[:count], *made, *rest)

    extra = [*slots, pltpu.SemaphoreType.DMA((len(raw),))] if raw else []
    return pl.pallas_call(
        run,
        out_shape=outs,
        in_specs=specs,
        out_specs=[pl.BlockSpec(memory_space=pltpu.VMEM)] * len(outs),
        scratch_shapes=[*scratch, *extra],
        compiler_params=pltpu.CompilerParams(vmem_limit_bytes=VMEM_LIMIT),
    )(*near, *far, *scalars, *waits)


def lanes():
    return lax.broadcasted_iota(jnp.int32, (8, 128), 1)


def spread(flat, values):
    channels, rows, cols = values.shape
    for t in range(cols // 128):
        part = values[:, :, t * 128 : t * 128 + 128]
        flat[t] = part.reshape(channels * rows, 128)


def gather(flat, channels, rows):
    parts = [flat[t].reshape(channels, rows, 128) for t in range(flat.shape[0])]
    return jnp.concatenate(parts, axis=2)


def row_of(flat, i, channels, rows):
    parts = [flat[t, pl.ds(i, channels, stride=rows), :] for t in range(flat.shape[0])]
    return jnp.concatenate(parts, axis=1)


def choose(flag, yes, no):
    return jnp.where(jnp.broadcast_to(flag, yes.shape) > 0, yes, no)


def split_ends(m_ref, even, inner_ref, outer_ref):
    rows = m_ref.shape[0]
    for k in range(RING):
        first, last = m_ref[k].astype(F32), m_ref[rows - RING + k].astype(F32)
        inner_ref[k] = choose(even, last, first).astype(BF16)
        outer_ref[k] = choose(even, first, last).astype(BF16)


def rows_body(settle, f_ref, mask_ref, place_ref, m_ref, inner_ref, outer_ref, flat):
    channels, rows, cols = f_ref.shape
    settle()
    spread(flat, f_ref[...].astype(F32) * mask_ref[...].astype(F32)[None])
    for i in range(rows):
        m_ref[i] = row_of(flat, i, channels, rows).astype(BF16)
    split_ends(m_ref, place_ref[0], inner_ref, outer_ref)


def strips_body(
    m_ref, outer_ref, inner_ref, place_ref, south_ref, halo_ref, near_ref, far_ref
):
    rows, channels, cols = m_ref.shape
    here = lax.broadcasted_iota(jnp.int32, (cols, cols), 0)
    there = lax.broadcasted_iota(jnp.int32, (cols, cols), 1)
    flip = (here + there == cols - 1).astype(F32).astype(BF16)
    even, top, lon_even = place_ref[0], place_ref[1], place_ref[2]
    for k in range(RING):
        inner = inner_ref[k].astype(F32)
        outer = outer_ref[k].astype(F32)
        turned = jnp.dot(outer_ref[RING - 1 - k], flip, preferred_element_type=F32)
        south_ref[k] = choose(even, outer, inner).astype(BF16)
        halo_ref[k] = choose(even, inner, choose(top, turned, outer)).astype(BF16)
    lane = lax.broadcasted_iota(jnp.int32, (channels, 128), 1)
    left = jnp.zeros((channels, 128), F32)
    right = jnp.zeros((channels, 128), F32)
    for r in range(rows + 2 * RING):
        if r < RING:
            ref, at = south_ref, r
        elif r < rows + RING:
            ref, at = m_ref, r - RING
        else:
            ref, at = halo_ref, r - RING - rows
        here = (lane >= RING * r) & (lane < RING * r + RING)
        head = ref[at, :, 0:128].astype(F32)
        tail = ref[at, :, cols - 128 : cols].astype(F32)
        if r:
            head = pltpu.roll(head, RING * r, 1)
        tail = pltpu.roll(tail, RING * r + RING, 1)
        left = jnp.where(here, head, left)
        right = jnp.where(here, tail, right)
    near_ref[...] = choose(lon_even, right, left).astype(BF16)
    far_ref[...] = choose(lon_even, left, right).astype(BF16)


def strips_and_sums_body(
    m_ref, outer_ref, inner_ref, sums_ref, place_ref,
    south_ref, halo_ref, near_ref, far_ref, out_ref,
):
    strips_body(
        m_ref, outer_ref, inner_ref, place_ref, south_ref, halo_ref, near_ref, far_ref
    )
    out_ref[...] = sums_ref[...]


def fill(ext, m_ref, south_ref, halo_ref, near_ref, far_ref, lon_even):
    rows, channels, cols = m_ref.shape
    lane = lax.broadcasted_iota(jnp.int32, (channels, 128), 1)
    near = near_ref[...].astype(F32)
    far = far_ref[...].astype(F32)
    before = choose(lon_even, far, near)
    after = choose(lon_even, near, far)
    for r in range(rows + 2 * RING):
        if r < RING:
            row = south_ref[r]
        elif r < rows + RING:
            row = m_ref[r - RING]
        else:
            row = halo_ref[r - RING - rows]
        ext[r, :, 0:cols] = row.astype(F32)
        right = after if r == 0 else pltpu.roll(after, 128 - RING * r, 1)
        left = pltpu.roll(before, 128 - RING - RING * r, 1)
        ext[r, :, cols : cols + 128] = jnp.where(
            lane < RING, right, jnp.where(lane >= 128 - RING, left, 0.0)
        )


def windows(tiles, step, lane):
    if step == 0:
        return tiles[:-1]
    count = len(tiles)
    shift = 128 - step if step > 0 else -step
    turned = [jnp.zeros((8, 128), F32) if t is None else pltpu.roll(t, shift, 1) for t in tiles]
    if step > 0:
        keep = lane < 128 - step
        return [jnp.where(keep, turned[t], turned[t + 1]) for t in range(count - 1)]
    keep = lane >= -step
    return [jnp.where(keep, turned[t], turned[t - 1]) for t in range(count - 1)]


def tap_columns(dw_ref):
    rows = jnp.concatenate([dw_ref[a] for a in range(7)], axis=0)
    blank = jnp.zeros((128 - rows.shape[0], rows.shape[1]), F32)
    return jnp.concatenate([rows, blank], axis=0).T


def tap_tiles(taps, c0):
    return lambda index: taps[index, pl.ds(c0, 8), :]


def correlate(read, span, rows, lane, weights, flipped, top, summed):
    for b in range(7):
        taps = [weights(48 - a * 7 - b if flipped else a * 7 + b) for a in range(7)]
        far = taps
        if top is not None:
            far = [jnp.where(top, weights(a * 7 + b), taps[a]) for a in range(7)]
        for r in span:
            wins = windows(read(r), b - RING, lane)
            for a in range(7):
                i = r - a
                if 0 <= i < rows:
                    weight = far[a] if r >= rows + RING else taps[a]
                    for t, win in enumerate(wins):
                        term = weight * win
                        old = summed[i][t]
                        summed[i][t] = term if old is None else old + term
    return summed


def edges(before, after, rows, lane, weights, flipped, top):
    spot = lane % RING
    left = jnp.zeros((8, 128), F32)
    right = jnp.zeros((8, 128), F32)
    for a in range(7):
        for b in (0, 1, 2, 4, 5, 6):
            weight = weights(48 - a * 7 - b if flipped else a * 7 + b)
            if top is not None and a > RING:
                beyond = top & (lane >= RING * (rows + RING - a))
                weight = jnp.where(beyond, weights(a * 7 + b), weight)
            back = -(RING * a + b) % 128 if b < RING else -(RING * a + b - 6) % 128
            strip = before if b < RING else after
            moved = pltpu.roll(strip, back, 1) if back else strip
            if b < RING:
                left = left + jnp.where(spot <= 2 - b, weight * moved, 0.0)
            else:
                right = right + jnp.where(spot >= 6 - b, weight * moved, 0.0)
    return left, right


def place_edges(left, right, i, lane):
    head = pltpu.roll(left, 128 - RING * i, 1) if i else left
    tail = pltpu.roll(right, 128 - RING - RING * i, 1)
    return jnp.where(lane < RING, head, 0.0), jnp.where(lane >= 128 - RING, tail, 0.0)


def spread_taps(dw_ref, taps_ref):
    columns = tap_columns(dw_ref)
    for k in range(49):
        taps_ref[k] = jnp.broadcast_to(columns[:, k : k + 1], columns.shape)


def first_body(flipped, settle, m_ref, dw_ref, conv_ref, taps_ref, wide):
    settle()
    spread_taps(dw_ref, taps_ref)
    own_body(flipped, m_ref, taps_ref, conv_ref, wide)


def own_body(flipped, m_ref, taps, conv_ref, wide):
    rows, channels, cols = m_ref.shape
    pairs = cols // 128
    wide[...] = m_ref[...].astype(F32)

    def step(ct, carry):
        c0 = pl.multiple_of(ct * 8, 8)

        def read(r):
            tiles = [wide[r - RING, pl.ds(c0, 8), t * 128 : t * 128 + 128] for t in range(pairs)]
            return tiles + [None]

        blank = [[None] * pairs for _ in range(rows)]
        span = range(RING, rows + RING)
        weights = tap_tiles(taps, c0)
        summed = correlate(read, span, rows, lanes(), weights, flipped, None, blank)
        for i in range(rows):
            for t in range(pairs):
                conv_ref[i, pl.ds(c0, 8), t * 128 : t * 128 + 128] = summed[i][t]
        return carry

    lax.fori_loop(0, channels // 8, step, 0)


def with_ends(conv_ref, wide, c0, lane, weights, flipped, top):
    rows, channels, cols = conv_ref.shape
    pairs = cols // 128

    def read(r):
        at = r if r < RING else r - rows
        tiles = [wide[at, pl.ds(c0, 8), t * 128 : t * 128 + 128] for t in range(pairs)]
        return tiles + [None]

    summed = [
        [conv_ref[i, pl.ds(c0, 8), t * 128 : t * 128 + 128] for t in range(pairs)]
        for i in range(rows)
    ]
    span = [*range(RING), *range(rows + RING, rows + 2 * RING)]
    return correlate(read, span, rows, lane, weights, flipped, top, summed)


def ends_body(south_ref, halo_ref, conv_ref, taps, out_ref, wide):
    rows, channels, cols = conv_ref.shape
    wide[0:RING] = south_ref[...].astype(F32)
    wide[RING : 2 * RING] = halo_ref[...].astype(F32)

    def step(ct, carry):
        c0 = pl.multiple_of(ct * 8, 8)
        weights = tap_tiles(taps, c0)
        summed = with_ends(conv_ref, wide, c0, lanes(), weights, False, None)
        for i in range(rows):
            for t in range(cols // 128):
                out_ref[i, pl.ds(c0, 8), t * 128 : t * 128 + 128] = summed[i][t]
        return carry

    lax.fori_loop(0, channels // 8, step, 0)


def split_sides(sides, near_ref, far_ref, lon_even):
    near = near_ref[...].astype(F32)
    far = far_ref[...].astype(F32)
    sides[0] = choose(lon_even, far, near)
    sides[1] = choose(lon_even, near, far)


def block_body(
    settle, m_ref, conv_ref, far_ref, near_ref, taps, ct_ref, mask_ref,
    gain_ref, w_in_ref, b_ref, w_out_ref, place_ref,
    out_ref, g_ref, inner_ref, outer_ref, wide_ref, tail_ref,
    conv, flat, act, back, sca, pre, b_acc, gain_acc, sides,
):
    rows, channels, cols = m_ref.shape
    hidden = w_out_ref.shape[0]
    pairs = cols // 128
    split_sides(sides, near_ref, far_ref, place_ref[2])
    settle()
    sea = mask_ref[...].astype(F32)
    spread(flat, ct_ref[...].astype(F32) * sea[None])
    for i in range(rows):
        back[:, i * cols : i * cols + cols] = row_of(flat, i, channels, rows).astype(BF16)

    def conv_step(ct, carry):
        c0 = pl.multiple_of(ct * 8, 8)
        lane = lanes()
        before, after = sides[0, pl.ds(c0, 8), :], sides[1, pl.ds(c0, 8), :]
        weights = tap_tiles(taps, c0)
        left, right = edges(before, after, rows, lane, weights, False, None)
        for i in range(rows):
            head, tail = place_edges(left, right, i, lane)
            for t in range(pairs):
                tile = conv_ref[i, pl.ds(c0, 8), t * 128 : t * 128 + 128]
                if t == 0:
                    tile = tile + head
                if t == pairs - 1:
                    tile = tile + tail
                conv[i, pl.ds(c0, 8), t * 128 : t * 128 + 128] = tile
        return carry

    lax.fori_loop(0, channels // 8, conv_step, 0)

    b_acc[...] = jnp.zeros_like(b_acc)
    gain_acc[...] = jnp.zeros_like(gain_acc)
    gain = jnp.broadcast_to(gain_ref[...], (128, channels)).T
    gain = jnp.concatenate([gain] * pairs, axis=1)
    bias = jnp.broadcast_to(b_ref[...], (128, hidden)).T
    bias = jnp.concatenate([bias] * pairs, axis=1)
    w_in_t = w_in_ref[...].T
    w_out_t = w_out_ref[...].T
    root = 0.7978845608028654
    for i in range(rows):
        span = slice(i * cols, i * cols + cols)
        raw = conv[i]
        centred = raw - jnp.mean(raw, axis=0, keepdims=True)
        inv_std = lax.rsqrt(jnp.mean(centred * centred, axis=0, keepdims=True) + 1e-06)
        normed = centred * inv_std
        scaled = (normed * gain).astype(BF16)
        sca[:, span] = scaled
        v = jnp.dot(w_in_t, scaled, preferred_element_type=F32) + bias
        v2 = v * v
        t = jnp.tanh(root * v * (1.0 + 0.044715 * v2))
        half = 0.5 * (1.0 + t)
        activated = (v * half).astype(BF16)
        act[:, span] = activated
        slope = half + 0.5 * v * (1.0 - t * t) * (root * (1.0 + 3 * 0.044715 * v2))
        mixed = jnp.dot(w_out_t, activated, preferred_element_type=F32)
        mixed = m_ref[i].astype(F32) + mixed
        for t in range(pairs):
            flat[t, pl.ds(i, channels, stride=rows), :] = mixed[:, t * 128 : t * 128 + 128]
        act_grad = jnp.dot(w_out_ref[...], back[:, span], preferred_element_type=F32)
        pre_grad = (act_grad * slope).astype(BF16)
        pre[:, span] = pre_grad
        wide = pre_grad.astype(F32)
        b_acc[...] += sum(wide[:, t * 128 : t * 128 + 128] for t in range(pairs))
        scaled_grad = jnp.dot(w_in_ref[...], pre_grad, preferred_element_type=F32)
        gains = scaled_grad * normed
        gain_acc[...] += sum(gains[:, t * 128 : t * 128 + 128] for t in range(pairs))
        norm_grad = scaled_grad * gain
        grad = inv_std * (
            norm_grad
            - jnp.mean(norm_grad, axis=0, keepdims=True)
            - normed * jnp.mean(norm_grad * normed, axis=0, keepdims=True)
        )
        g_ref[i] = grad.astype(BF16)

    split_ends(g_ref, place_ref[0], inner_ref, outer_ref)
    out_ref[...] = (gather(flat, channels, rows) * sea[None]).astype(BF16)
    over_cells = (((1,), (1,)), ((), ()))
    w_in_sum = lax.dot_general(sca[...], pre[...], over_cells, preferred_element_type=F32)
    w_out_sum = lax.dot_general(act[...], back[...], over_cells, preferred_element_type=F32)
    low = channels + hidden
    shift = hidden - 128
    wide_ref[0:channels, :] = w_in_sum[:, 0:128].astype(BF16)
    blank = jnp.zeros((hidden, 128 - channels), F32)
    wide_ref[channels:low, :] = jnp.concatenate([w_out_sum, blank], axis=1).astype(BF16)
    blank = jnp.zeros((channels, 128 - shift), F32)
    tail = jnp.concatenate([w_in_sum[:, 128:hidden], blank], axis=1)
    lane = lax.broadcasted_iota(jnp.int32, (channels, 128), 1)
    tail = jnp.where(lane == shift + 49, jnp.sum(gain_acc[...], axis=1, keepdims=True), tail)
    for part in range(hidden // channels):
        column = jnp.sum(b_acc[part * channels : part * channels + channels, :], axis=1, keepdims=True)
        tail = jnp.where(lane == shift + 50 + part, column, tail)
    tail_ref[...] = tail


def kernel_body(
    shift, m_ref, south_ref, halo_ref, near_ref, far_ref, g_ref, wide_ref, tail_ref, place_ref,
    sums_ref, tail, grid, ext, held_sums,
):
    rows, channels, cols = g_ref.shape
    pairs = cols // 128
    fill(ext, m_ref, south_ref, halo_ref, near_ref, far_ref, place_ref[2])
    grid[...] = g_ref[...].astype(F32)

    def kernel_step(ct, carry):
        c0 = pl.multiple_of(ct * 8, 8)
        lane = lanes()
        grads = [
            [grid[i, pl.ds(c0, 8), t * 128 : t * 128 + 128] for t in range(pairs)]
            for i in range(rows)
        ]
        for b in range(7):
            summed = [None] * 7
            for r in range(rows + 2 * RING):
                tiles = [ext[r, pl.ds(c0, 8), t * 128 : t * 128 + 128] for t in range(pairs + 1)]
                wins = windows(tiles, b - RING, lane)
                for a in range(7):
                    i = r - a
                    if 0 <= i < rows:
                        for t in range(pairs):
                            term = grads[i][t] * wins[t]
                            summed[a] = term if summed[a] is None else summed[a] + term
            for a in range(7):
                held_sums[a * 7 + b, pl.ds(c0, 8), :] = summed[a]
        return carry

    lax.fori_loop(0, channels // 8, kernel_step, 0)
    tail[...] = tail_ref[...]
    lane = lax.broadcasted_iota(jnp.int32, (channels, 128), 1)
    ones = jnp.ones((256, 128), BF16)
    for k in range(49):
        high = held_sums[k].astype(BF16)
        low_part = (held_sums[k] - high.astype(F32)).astype(BF16)
        both = jnp.concatenate([high, low_part], axis=1)
        over_lanes = jnp.dot(both, ones, preferred_element_type=F32)
        tail[...] = jnp.where(lane == shift + k, over_lanes, tail[...])
    low = wide_ref.shape[0]
    sums_ref[0:low, :] = wide_ref[...]
    sums_ref[low : low + channels, :] = tail[...].astype(BF16)


def back_body(
    settle, conv_ref, south_ref, halo_ref, near_ref, far_ref, ct_ref, mask_ref, dw_ref, place_ref,
    out_ref, wide, flat, sides, taps,
):
    rows, channels, cols = conv_ref.shape
    pairs = cols // 128
    wide[0:RING] = south_ref[...].astype(F32)
    wide[RING : 2 * RING] = halo_ref[...].astype(F32)
    split_sides(sides, near_ref, far_ref, place_ref[2])
    settle()
    spread_taps(dw_ref, taps)

    def step(ct, carry):
        c0 = pl.multiple_of(ct * 8, 8)
        lane = lanes()
        top = jnp.broadcast_to(place_ref[1], (8, 128)) > 0
        weights = tap_tiles(taps, c0)
        before, after = sides[0, pl.ds(c0, 8), :], sides[1, pl.ds(c0, 8), :]
        left, right = edges(before, after, rows, lane, weights, True, top)
        summed = with_ends(conv_ref, wide, c0, lane, weights, True, top)
        for i in range(rows):
            head, tail = place_edges(left, right, i, lane)
            for t in range(pairs):
                tile = summed[i][t]
                if t == 0:
                    tile = tile + head
                if t == pairs - 1:
                    tile = tile + tail
                flat[t, pl.ds(c0 * rows + i, 8, stride=rows), :] = tile
        return carry

    lax.fori_loop(0, channels // 8, step, 0)
    sea = mask_ref[...].astype(F32)[None]
    grad = gather(flat, channels, rows) + ct_ref[...].astype(F32) * sea
    out_ref[...] = (grad * sea).astype(BF16)


def lat_halo(inner, outer):
    n_lat, n_lon = lax.axis_size("lat"), lax.axis_size("lon")
    pairs = []
    for i in range(n_lon):
        for j in range(1, n_lat - 1, 2):
            pairs += [(i * n_lat + j, i * n_lat + j + 1), (i * n_lat + j + 1, i * n_lat + j)]
        pairs.append((i * n_lat + n_lat - 1, (n_lon - 1 - i) * n_lat + n_lat - 1))
    outer = lax.ppermute(outer, ("lon", "lat"), pairs)
    inner = lax.ppermute(inner, "lat", [(i, i ^ 1) for i in range(n_lat)])
    return inner, outer


def lon_halo(near, far):
    n_lon = lax.axis_size("lon")
    far = lax.ppermute(far, "lon", [(i, (i - 1 + 2 * (i % 2)) % n_lon) for i in range(n_lon)])
    near = lax.ppermute(near, "lon", [(i, i ^ 1) for i in range(n_lon)])
    return near, far


def held(struct):
    return pltpu.VMEM(struct.shape, struct.dtype)


def like(shape, dtype):
    return jax.ShapeDtypeStruct(shape, dtype)


def spread_body(pieces_ref, out_ref):
    summed = jnp.sum(pieces_ref[...].astype(F32), axis=0).astype(out_ref.dtype)
    for i in range(out_ref.shape[0]):
        out_ref[i] = summed


def unpack_body(scale, sums_ref, w_in_ref, w_out_ref, dw_ref, gain_ref, b_ref):
    channels, hidden = w_in_ref.shape
    low = channels + hidden
    shift = hidden - 128
    tail = sums_ref[low : low + channels, :] * scale
    w_in_ref[...] = jnp.concatenate([sums_ref[0:channels, :] * scale, tail[:, 0:shift]], axis=1)
    w_out_ref[...] = sums_ref[channels:low, 0:channels] * scale
    turned = tail.T
    for a in range(7):
        dw_ref[a] = turned[shift + 7 * a : shift + 7 * a + 7, :]
    gain_ref[...] = turned[shift + 49 : shift + 50, :]
    parts = [turned[shift + 50 + k : shift + 51 + k, :] for k in range(hidden // channels)]
    b_ref[...] = jnp.concatenate(parts, axis=1)


def shards(fields, land_mask, dw_kernel, gain, w_in, b_in, w_out, cotangent):
    channels, rows, cols = fields.shape
    hidden = w_out.shape[0]
    n_lat, n_lon = lax.axis_size("lat"), lax.axis_size("lon")
    taps = dw_kernel.transpose(1, 2, 0)
    lat, lon = lax.axis_index("lat"), lax.axis_index("lon")
    place = jnp.stack([1 - lat % 2, (lat == n_lat - 1).astype(jnp.int32), 1 - lon % 2])
    ring = like((RING, channels, cols), BF16)
    grid = like((rows, channels, cols), BF16)
    whole = like((channels, rows, cols), BF16)
    flat = pltpu.VMEM((cols // 128, channels * rows, 128), F32)
    ext = pltpu.VMEM((rows + 2 * RING, channels, cols + 128), F32)
    near_ring = held(ring)
    strip = pltpu.VMEM((channels, 128), BF16)
    height = 2 * channels + hidden
    near_sums = pltpu.VMEM((height, 128), BF16)
    cells = rows * cols
    masked, inner, outer = call(
        rows_body, [held(grid), near_ring, near_ring], [], [fields, land_mask], [place],
        scratch=[flat],
    )
    inner, outer = lat_halo(inner, outer)
    columns = pltpu.VMEM((channels, 128), F32)
    sides = pltpu.VMEM((2, channels, 128), F32)
    sums_grid = pltpu.VMEM((rows, channels, cols), F32)
    ends = pltpu.VMEM((2 * RING, channels, cols), F32)
    tap_grid = pltpu.VMEM((49, channels, 128), F32)
    conv, tiles = call(
        functools.partial(first_body, False), [sums_grid, tap_grid], [masked], [taps],
        scratch=[sums_grid],
    )
    south, north, near, far = call(
        strips_body, [near_ring, near_ring, strip, strip], [masked, outer, inner], (), [place],
        waits=[conv],
    )
    near, far = lon_halo(near, far)
    (conv,) = call(
        ends_body, [sums_grid], [south, north, conv, tiles], scratch=[ends]
    )
    output, grads, inner, outer, wide, tail = call(
        block_body,
        [
            whole, held(grid), near_ring, near_ring,
            pltpu.VMEM((height - channels, 128), BF16), columns,
        ],
        [masked, conv, far, near, tiles],
        [
            cotangent, land_mask, gain.reshape(1, channels), w_in,
            b_in.reshape(1, hidden), w_out,
        ],
        [place],
        scratch=[
            pltpu.VMEM((rows, channels, cols), F32),
            flat,
            pltpu.VMEM((hidden, cells), BF16),
            pltpu.VMEM((channels, cells), BF16),
            pltpu.VMEM((channels, cells), BF16),
            pltpu.VMEM((hidden, cells), BF16),
            pltpu.VMEM((hidden, 128), F32),
            columns,
            sides,
        ],
    )
    inner, outer = lat_halo(inner, outer)
    (sums,) = call(
        functools.partial(kernel_body, hidden - 128), [near_sums],
        [masked, south, north, near, far, grads, wide, tail], (), [place],
        scratch=[columns, sums_grid, ext, tap_grid],
    )
    south, north, near, far, sums = call(
        strips_and_sums_body, [near_ring, near_ring, strip, strip, near_sums],
        [grads, outer, inner, sums], (), [place],
    )
    size = height // n_lat
    pieces = lax.all_to_all(sums.reshape(n_lat, size, 128), "lat", 0, 0, tiled=True)
    (conv,) = call(
        functools.partial(first_body, True), [sums_grid], [grads], [taps],
        scratch=[tap_grid, sums_grid], waits=[near],
    )
    near, far = lon_halo(near, far)
    (pieces,) = call(
        spread_body, [pltpu.VMEM((n_lon, size, 128), BF16)], [pieces], waits=[conv, near]
    )
    pieces = lax.all_to_all(pieces, "lon", 0, 0, tiled=True)
    (pieces,) = call(
        spread_body, [pltpu.VMEM((n_lat, size, 128), F32)], [pieces], waits=[far]
    )
    pieces = lax.all_to_all(pieces, "lat", 0, 0, tiled=True)
    (input_grad,) = call(
        back_body, [whole], [conv, south, north, near, far], [cotangent, land_mask, taps],
        [place], scratch=[ends, flat, sides, tap_grid],
    )
    scale = float(cells * n_lat * n_lon) ** -0.5
    w_in_grad, w_out_grad, dw_grad, gain_grad, b_grad = call(
        functools.partial(unpack_body, scale),
        [
            like((channels, hidden), F32),
            like((hidden, channels), F32),
            like((7, 7, channels), F32),
            like((1, channels), F32),
            like((1, hidden), F32),
        ],
        [pieces.reshape(height, 128)],
    )
    return (
        output,
        input_grad,
        dw_grad.transpose(2, 0, 1),
        gain_grad.reshape(channels),
        w_in_grad,
        b_grad.reshape(hidden),
        w_out_grad,
    )


def solution(mesh):
    tiles = P(None, "lat", "lon")
    return jax.shard_map(
        shards,
        mesh=mesh,
        in_specs=(tiles, P("lat", "lon"), P(), P(), P(), P(), P(), tiles),
        out_specs=(tiles, tiles, P(), P(), P(), P(), P()),
        check_vma=False,
    )
```
